256 devices in a mesh: rows: 32 (over z, x), cols: 8 (over y, core).
Axes of the slice: x: 4, y: 4, z: 8, core: 2. Of those that a mesh axis runs over, the one named last changes fastest.
Arguments:
- panel: float32 [131072, 256], P('rows'), may hold values from -0.099436891 to 0.099436891
- trailing: float32 [131072, 1024], P('rows', 'cols'), may hold values from -6 to 6
Outputs:
- factor_r: float32 [256, 256], replicated
- projected: float32 [256, 1024], P(None, 'cols')
- remainder: float32 [131072, 1024], P('rows', 'cols')
The draws below stay inside these ranges and needn't reach their ends.
All inputs are finite; a program needn't handle non-finite values.
Results may differ from the reference program's by a relative error of at most 0.0003.
Values sent between devices are 32-bit elements; how exact they have to be, the bound alone decides.
No kernel may reach another device: no remote copies, remote signals or barrier semaphores. Data moves between devices by JAX's collectives and lax.ppermute only.
A program may use at most 64 MiB of HBM per device.

```python
import jax
import jax.numpy as jnp
from jax import lax

PANEL = 256
TRAIL = 1024
NROWS = 131072


def draw_panel(key, part):
    key = jax.random.fold_in(key, 11)
    key_shared, key_own, key_spread, key_scale = jax.random.split(key, 4)
    groups = 8
    position = jnp.arange(NROWS, dtype=jnp.float32) / (NROWS - 1)
    reach = 3.0
    shared = jnp.clip(jax.random.normal(key_shared, (NROWS, groups), jnp.float32), -reach, reach)
    own = jnp.clip(jax.random.normal(key_own, (NROWS, PANEL), jnp.float32), -reach, reach)
    rising = 1.0 + 2.0 * position
    lowest = 0.006
    shared = shared.at[NROWS - 1, 0].set(reach).at[NROWS - 1, 1].set(-reach)
    own = own.at[NROWS - 1, 0].set(reach).at[NROWS - 1, 1].set(-reach)
    spread = jnp.exp(jax.random.uniform(key_spread, (PANEL,), jnp.float32, jnp.log(lowest), 0.0))
    spread = spread.at[0].set(1.0).at[1].set(1.0)
    column_scale = jnp.exp(jax.random.uniform(key_scale, (PANEL,), jnp.float32, jnp.log(0.5), jnp.log(2.0)))
    column_scale = column_scale.at[0].set(2.0).at[1].set(2.0)
    common = jnp.tile(shared, (1, PANEL // groups))
    mixed = common + spread[None, :] * own
    scaled = mixed * column_scale[None, :] * rising[:, None] / jnp.sqrt(jnp.float32(NROWS))
    return scaled.astype(jnp.float32)


def steps_of(rng, extent, shards, least, largest):
    factor_of = 1.0
    for dim, blocks in shards:
        steps = jax.random.uniform(jax.random.fold_in(jax.random.fold_in(rng, 6), dim), (blocks,), jnp.float32, least / len(shards), largest / len(shards))
        factor_of = factor_of * jnp.repeat(jnp.exp(steps), extent[dim] // blocks).reshape((-1,) + (1,) * (len(extent) - 1 - dim))
    return factor_of


def centred(stream_key, extent, scale, most, pieces=(), kind=jnp.bfloat16):
    array = jax.random.normal(stream_key, extent, jnp.float32) * scale
    if len(pieces) > 0:
        array = steps_of(stream_key, extent, pieces, -0.22, 0.18) * array
    return jnp.clip(array, min=-most, max=most).astype(kind)


def setup_inputs(seed: int = 0) -> dict:
    keys = jax.random.split(jax.random.key(seed), 3)
    panel = draw_panel(jax.random.fold_in(keys[2], 71), 0)
    trailing = centred(keys[1], (NROWS, TRAIL), 1.0, 6.0, ((0, 32), (1, 8)), jnp.float32)
    return dict(panel=panel, trailing=trailing)


def reference(panel, trailing):
    basis, factor = jnp.linalg.qr(panel)
    signs = jnp.sign(jnp.diagonal(factor))
    factor_r = factor * signs[:, None]
    basis = basis * signs[None, :]
    projected = jnp.dot(basis.T.astype(jnp.float32), trailing.astype(jnp.float32), precision=lax.Precision.HIGHEST, preferred_element_type=jnp.float32)
    remainder = trailing - jnp.dot(basis.astype(jnp.float32), projected.astype(jnp.float32), precision=lax.Precision.HIGHEST, preferred_element_type=jnp.float32)
    return (factor_r, projected, remainder)
```

```python
import jax
import jax.numpy as jnp
from jax import lax
from jax.experimental import pallas as pl
from jax.experimental.pallas import tpu as pltpu
from jax.sharding import PartitionSpec as P

F32 = jnp.float32
BF16 = jnp.bfloat16
N = 256
H = 128
RING = 32
VMEM = 48 * 1024 * 1024


def dot_t(a, b):
    return lax.dot_general(a, b, (((0,), (0,)), ((), ())), preferred_element_type=F32)


def dot_n(a, b):
    return lax.dot_general(a, b, (((1,), (0,)), ((), ())), preferred_element_type=F32)


def dot_r(a, b):
    return lax.dot_general(a, b, (((1,), (1,)), ((), ())), preferred_element_type=F32)


def split3(x):
    one = x.astype(BF16)
    rest = x - one.astype(F32)
    two = rest.astype(BF16)
    three = (rest - two.astype(F32)).astype(BF16)
    return one, two, three


def product6(dot, a, b):
    a1, a2, a3 = split3(a)
    b1, b2, b3 = split3(b)
    small = (dot(a1, b3) + dot(a3, b1)) + dot(a2, b2)
    return dot(a1, b1) + ((dot(a1, b2) + dot(a2, b1)) + small)


def power_near(x):
    big = x * F32(2.0**23 + 1.0)
    return big - (big - x)


def grid_split(x, bits):
    top = jnp.max(jnp.abs(x), axis=0, keepdims=True)
    magic = power_near(top) * F32(1.5 * 2.0 ** (23 - bits))
    coarse = (x + magic) - magic
    rest = x - coarse
    two = rest.astype(BF16)
    three = (rest - two.astype(F32)).astype(BF16)
    return coarse.astype(BF16), two, three


def two_sum(a, b):
    s = a + b
    t = s - a
    return s, (a - (s - t)) + (b - t)


def gram_kernel(panel_ref, trailing_ref, out_ref, hi, lo, cross, proj):
    step = pl.program_id(0)

    @pl.when(step == 0)
    def _():
        hi[...] = jnp.zeros_like(hi)
        lo[...] = jnp.zeros_like(lo)
        cross[...] = jnp.zeros_like(cross)
        proj[...] = jnp.zeros_like(proj)

    a1, a2, a3 = grid_split(panel_ref[...], 6)
    t1, t2, t3 = split3(trailing_ref[...])
    exact = dot_t(a1, a1)
    half = a2 * BF16(0.5)
    cross[...] += (dot_t(a1, a2) + dot_t(a1, a3)) + (dot_t(a2, half) + dot_t(a2, a3))
    proj[...] += dot_t(a1, t1) + (
        (dot_t(a1, t2) + dot_t(a2, t1)) + ((dot_t(a1, t3) + dot_t(a3, t1)) + dot_t(a2, t2))
    )
    s, e = two_sum(hi[...], exact)
    hi[...] = s
    lo[...] += e

    @pl.when(step == pl.num_programs(0) - 1)
    def _():
        v = cross[...]
        c = v + v.T
        s, e = two_sum(hi[...], c)
        hi[...] = s
        lo[...] += e
        for d in range(RING):
            for k in range(3):
                r0 = 12 * d + 4 * k
                rows = slice(r0 % H + (0 if r0 < H else H), r0 % H + (0 if r0 < H else H) + 4)
                cols = slice(0, H) if r0 < 2 * H else slice(H, N)
                out_ref[d, 4 * k : 4 * k + 4, :] = hi[rows, cols]
                out_ref[d, 12 + 4 * k : 16 + 4 * k, :] = lo[rows, cols]
            out_ref[d, 24:32, :] = proj[8 * d : 8 * d + 8, :]


def gram(panel, trailing):
    rows = panel.shape[0]
    chunk = 1024
    return pl.pallas_call(
        gram_kernel,
        grid=(rows // chunk,),
        in_specs=[
            pl.BlockSpec((chunk, N), lambda i: (i, 0)),
            pl.BlockSpec((chunk, H), lambda i: (i, 0)),
        ],
        out_specs=pl.BlockSpec((RING, 32, H), lambda i: (0, 0, 0)),
        out_shape=jax.ShapeDtypeStruct((RING, 32, H), F32),
        scratch_shapes=[
            pltpu.VMEM((N, N), F32),
            pltpu.VMEM((N, N), F32),
            pltpu.VMEM((N, N), F32),
            pltpu.VMEM((N, H), F32),
        ],
        compiler_params=pltpu.CompilerParams(vmem_limit_bytes=VMEM),
        name="products",
    )(panel, trailing)


def sum_kernel(in_ref, out_ref):
    parts = [(in_ref[d], None) for d in range(RING)]
    while len(parts) > 1:
        merged = []
        for (a, ea), (b, eb) in zip(parts[::2], parts[1::2]):
            s, e = two_sum(a, b)
            if ea is not None:
                e = e + (ea + eb)
            merged.append((s, e))
        parts = merged
    s, e = parts[0]
    hi, lo = two_sum(s[0:12], s[12:24] + e[0:12])
    out = jnp.concatenate([hi, lo, s[24:32] + e[24:32]], axis=0)
    out_ref[...] = jnp.broadcast_to(out[None], (RING, 32, H))


def sum_parts(received):
    return pl.pallas_call(
        sum_kernel,
        out_shape=jax.ShapeDtypeStruct((RING, 32, H), F32),
        compiler_params=pltpu.CompilerParams(vmem_limit_bytes=VMEM),
        name="sum_parts",
    )(received)


def factor_kernel(in_ref, factor_ref, proj_ref, coef_ref, hi, lo, c_ref, g, b):
    for d in range(RING):
        for k in range(3):
            r0 = 12 * d + 4 * k
            hi[r0 : r0 + 4, :] = in_ref[d, 4 * k : 4 * k + 4, :]
            lo[r0 : r0 + 4, :] = in_ref[d, 12 + 4 * k : 16 + 4 * k, :]
        c_ref[8 * d : 8 * d + 8, :] = in_ref[d, 24:32, :]
    g[0:H, 0:H] = hi[0:H, :]
    g[0:H, H:N] = hi[H : 2 * H, :].T
    g[H:N, 0:H] = jnp.zeros((H, H), F32)
    g[H:N, H:N] = hi[2 * H : 3 * H, :]
    row = lax.broadcasted_iota(jnp.int32, (N, N), 0)
    col = lax.broadcasted_iota(jnp.int32, (N, N), 1)
    b[...] = jnp.where(row == col, F32(1.0), F32(0.0))
    sub = lax.broadcasted_iota(jnp.int32, (8, H), 0)

    blocks = N // 8
    window = 3
    for t in range(blocks):
        groups = [(g, 0), (g, 1), (b, 0)] if t < blocks // 2 else [(g, 1), (b, 0), (b, 1)]
        wide = [w for w in range(window) if t + w < blocks]
        rows = [
            [ref[8 * (t + w) : 8 * (t + w) + 8, H * q : H * q + H] for ref, q in groups] for w in wide
        ]
        lane = (8 * t) % H
        if t < blocks // 2:
            pass
        x = [[None] * 8 for _ in wide]
        for w in wide:
            for k in range(8):
                if t < blocks // 2 and t + w >= blocks // 2:
                    piece = rows[0][1][:, (8 * (t + w)) % H : (8 * (t + w)) % H + 8].T
                    x[w][k] = jnp.broadcast_to(piece[:, k : k + 1], (8, H))
                else:
                    x[w][k] = jnp.broadcast_to(rows[w][0][:, lane + k : lane + k + 1], (8, H))
        for k in range(8):
            rs = lax.rsqrt(jnp.broadcast_to(x[0][k][k : k + 1, :], (8, H)))
            u = [x[w][k] * rs for w in wide]
            line = [jnp.broadcast_to(rows[0][q][k : k + 1, :], (8, H)) * rs for q in range(3)]
            for j in range(k + 1, 8):
                f = jnp.broadcast_to(u[0][j : j + 1, :], (8, H))
                for w in wide:
                    x[w][j] = x[w][j] - u[w] * f
            below = jnp.where(sub > k, u[0], F32(0.0))
            for q in range(3):
                rows[0][q] = jnp.where(sub == k, line[q], rows[0][q] - below * line[q])
                for w in wide[1:]:
                    rows[w][q] = rows[w][q] - u[w] * line[q]
        for w in wide:
            for q, (ref, p) in enumerate(groups):
                ref[8 * (t + w) : 8 * (t + w) + 8, H * p : H * p + H] = rows[w][q]
        first = 8 * (t + window)
        if first < N:
            u = jnp.concatenate(rows[0], axis=1)
            u1 = u.astype(BF16).astype(F32)
            r = u - u1
            u2 = r.astype(BF16).astype(F32)
            u3 = r - u2
            left = jnp.concatenate([u1, u1, u2, u1, u2, u3], axis=0).astype(BF16)
            right = jnp.concatenate([u1, u2, u1, u3, u2, u1], axis=0).astype(BF16)
            for half in range(2):
                lo_row, hi_row = max(first, H * half), H * half + H
                if lo_row >= hi_row:
                    continue
                q = [i for i, (ref, p) in enumerate(groups) if ref is g and p == half][0]
                change = dot_t(left[:, H * q : H * q + H], right)
                for i, (ref, p) in enumerate(groups):
                    if ref is g and p < half:
                        continue
                    ref[lo_row:hi_row, H * p : H * p + H] -= change[
                        lo_row - H * half :, H * i : H * i + H
                    ]

    upper = jnp.where(row <= col, g[...], F32(0.0))
    inverse = jnp.where(row >= col, b[...], F32(0.0))
    u1, u2, u3 = grid_split(upper, 7)
    exact = dot_t(u1, u1)
    v = (dot_t(u1, u2) + dot_t(u1, u3)) + (dot_t(u2, u2 * BF16(0.5)) + dot_t(u2, u3))
    v = v + v.T

    def left_of(ref, other):
        return (ref[0:H, :] - other[0:H, 0:H], ref[H : 2 * H, :] - other[H:N, 0:H], ref[2 * H : 3 * H, :] - other[H:N, H:N])

    d00, d10, d11 = left_of(hi, exact)
    d00 = (d00 + lo[0:H, :]) - v[0:H, 0:H]
    d10 = (d10 + lo[H : 2 * H, :]) - v[H:N, 0:H]
    d11 = (d11 + lo[2 * H : 3 * H, :]) - v[H:N, H:N]
    d = jnp.concatenate(
        [jnp.concatenate([d00, d10.T], axis=1), jnp.concatenate([d10, d11], axis=1)], axis=0
    )
    e = product6(dot_r, product6(dot_n, inverse, d), inverse)
    scale = jnp.where(row > col, F32(1.0), jnp.where(row == col, F32(0.5), F32(0.0)))
    x = e * scale

    def again(state):
        old, _, count = state
        new = (e - product6(dot_r, old, old)) * scale
        return new, jnp.max(jnp.abs(new - old)), count + 1

    x, _, _ = lax.while_loop(
        lambda s: jnp.logical_and(s[1] > F32(1e-6), s[2] < 20), again, (x, F32(1.0), jnp.int32(0))
    )
    factor_ref[...] = upper + product6(dot_t, x, upper)
    x2 = product6(dot_n, x, x)
    x4 = product6(dot_n, x2, x2)
    w = inverse - product6(dot_n, x, inverse)
    w = w + product6(dot_n, x2, w)
    w = w + product6(dot_n, x4, w)
    p = product6(dot_n, w, c_ref[...])
    proj_ref[...] = p
    coef_ref[...] = product6(dot_t, w, p)


def factor(gathered):
    return pl.pallas_call(
        factor_kernel,
        out_shape=(
            jax.ShapeDtypeStruct((N, N), F32),
            jax.ShapeDtypeStruct((N, H), F32),
            jax.ShapeDtypeStruct((N, H), F32),
        ),
        scratch_shapes=[
            pltpu.VMEM((3 * H, H), F32),
            pltpu.VMEM((3 * H, H), F32),
            pltpu.VMEM((N, H), F32),
            pltpu.VMEM((N, N), F32),
            pltpu.VMEM((N, N), F32),
        ],
        compiler_params=pltpu.CompilerParams(vmem_limit_bytes=VMEM),
        name="factor",
    )(gathered)


def remainder_kernel(panel_ref, trailing_ref, coef_ref, out_ref):
    out_ref[...] = trailing_ref[...] - product6(dot_n, panel_ref[...], coef_ref[...])


def remainder_of(panel, trailing, coef):
    rows = panel.shape[0]
    chunk = 512
    return pl.pallas_call(
        remainder_kernel,
        grid=(rows // chunk,),
        in_specs=[
            pl.BlockSpec((chunk, N), lambda i: (i, 0)),
            pl.BlockSpec((chunk, H), lambda i: (i, 0)),
            pl.BlockSpec((N, H), lambda i: (0, 0)),
        ],
        out_specs=pl.BlockSpec((chunk, H), lambda i: (i, 0)),
        out_shape=jax.ShapeDtypeStruct((rows, H), F32),
        compiler_params=pltpu.CompilerParams(vmem_limit_bytes=VMEM),
        name="remainder",
    )(panel, trailing, coef)


def on_device(panel, trailing):
    sent = gram(panel, trailing)
    received = lax.all_to_all(sent, "rows", 0, 0, tiled=True)
    summed = sum_parts(received)
    gathered = lax.all_to_all(summed, "rows", 0, 0, tiled=True)
    factor_r, projected, coef = factor(gathered)
    return factor_r, projected, remainder_of(panel, trailing, coef)


def solution(mesh):
    return jax.shard_map(
        on_device,
        mesh=mesh,
        in_specs=(P("rows", None), P("rows", "cols")),
        out_specs=(P(), P(None, "cols"), P("rows", "cols")),
        check_vma=False,
    )
```

```python
import jax
import jax.numpy as jnp
from jax import lax
from jax.experimental import pallas as pl
from jax.experimental.pallas import tpu as pltpu
from jax.sharding import PartitionSpec as P

F32 = jnp.float32
BF16 = jnp.bfloat16
N = 256
H = 128
RING = 32
VMEM = 48 * 1024 * 1024


def dot_t(a, b):
    return lax.dot_general(a, b, (((0,), (0,)), ((), ())), preferred_element_type=F32)


def dot_n(a, b):
    return lax.dot_general(a, b, (((1,), (0,)), ((), ())), preferred_element_type=F32)


def dot_r(a, b):
    return lax.dot_general(a, b, (((1,), (1,)), ((), ())), preferred_element_type=F32)


def split3(x):
    one = x.astype(BF16)
    rest = x - one.astype(F32)
    two = rest.astype(BF16)
    three = (rest - two.astype(F32)).astype(BF16)
    return one, two, three


def product6s(dot, a, b):
    small = (dot(a[0], b[2]) + dot(a[2], b[0])) + dot(a[1], b[1])
    return dot(a[0], b[0]) + ((dot(a[0], b[1]) + dot(a[1], b[0])) + small)


def product6(dot, a, b):
    return product6s(dot, split3(a), split3(b))


def power_near(x):
    big = x * F32(2.0**23 + 1.0)
    return big - (big - x)


def grid_split(x, bits):
    top = jnp.max(jnp.abs(x), axis=0, keepdims=True)
    magic = power_near(top) * F32(1.5 * 2.0 ** (23 - bits))
    coarse = (x + magic) - magic
    rest = x - coarse
    two = rest.astype(BF16)
    three = (rest - two.astype(F32)).astype(BF16)
    return coarse.astype(BF16), two, three


def two_sum(a, b):
    s = a + b
    t = s - a
    return s, (a - (s - t)) + (b - t)


CHUNK = 1024


def gram_kernel(core_ref, panel_hbm, trailing_hbm, out_ref, panel, trailing, sems):
    height = panel.shape[0]
    chunks = height // CHUNK

    def copies(i, start, size):
        rows = pl.ds(start, size)
        return (
            pltpu.make_async_copy(panel_hbm.at[rows], panel.at[rows], sems.at[0, i]),
            pltpu.make_async_copy(trailing_hbm.at[rows], trailing.at[rows], sems.at[1, i]),
        )

    first = copies(0, 0, CHUNK)
    later = copies(1, CHUNK, height - CHUNK)
    for copy in first + later:
        copy.start()
    first_core = core_ref[0] == 0

    def split(i):
        rows = slice(i * CHUNK, i * CHUNK + CHUNK)
        a = grid_split(panel[rows, :], 6)
        t = split3(trailing[rows, :])
        b = [
            jnp.concatenate([jnp.where(first_core, x[:, 0:H], x[:, H:N]), y], axis=1)
            for x, y in zip(a, t)
        ]
        return a, b

    for copy in first:
        copy.wait()
    held = split(0)
    for copy in later:
        copy.wait()
    hi = lo = rest = mixed = jnp.zeros((N, N), F32)
    for i in range(chunks):
        (a1, a2, a3), (b1, b2, b3) = held
        if i + 1 < chunks:
            held = split(i + 1)
        one = dot_t(a1, jnp.concatenate([b1, b2, b3], axis=1))
        two = dot_t(a2, jnp.concatenate([b1, b2, a3], axis=1))
        rest = rest + (one[:, N : 2 * N] + one[:, 2 * N :] + (two[:, 0:N] + two[:, N : 2 * N] + dot_t(a3, b1)))
        mixed = mixed + two[:, 2 * N :]
        hi, e = two_sum(hi, one[:, 0:N])
        lo = lo + e
    mixed = mixed + mixed.T
    s, e = two_sum(hi[:, 0:H], rest[:, 0:H] + jnp.where(first_core, mixed[:, 0:H], mixed[:, H:N]))
    out_ref[:, 0:8, :] = s.reshape(RING, 8, H)
    out_ref[:, 8:16, :] = (lo[:, 0:H] + e).reshape(RING, 8, H)
    out_ref[:, 16:24, :] = (hi[:, H:N] + (lo[:, H:N] + rest[:, H:N])).reshape(RING, 8, H)


def gram(core, panel, trailing):
    rows = panel.shape[0]
    return pl.pallas_call(
        gram_kernel,
        in_specs=[
            pl.BlockSpec(memory_space=pltpu.SMEM),
            pl.BlockSpec(memory_space=pl.ANY),
            pl.BlockSpec(memory_space=pl.ANY),
        ],
        out_specs=pl.BlockSpec(memory_space=pltpu.VMEM),
        out_shape=jax.ShapeDtypeStruct((RING, 24, H), F32),
        scratch_shapes=[
            pltpu.VMEM((rows, N), F32),
            pltpu.VMEM((rows, H), F32),
            pltpu.SemaphoreType.DMA((2, 2)),
        ],
        compiler_params=pltpu.CompilerParams(vmem_limit_bytes=60 * 1024 * 1024),
        name="products",
    )(core, panel, trailing)


def sum_kernel(in_ref, out_ref):
    parts = [(in_ref[d], None) for d in range(RING)]
    while len(parts) > 1:
        merged = []
        for (a, ea), (b, eb) in zip(parts[::2], parts[1::2]):
            s, e = two_sum(a, b)
            if ea is not None:
                e = e + (ea + eb)
            merged.append((s, e))
        parts = merged
    s, e = parts[0]
    hi, lo = two_sum(s[0:8], s[8:16] + e[0:8])
    out = jnp.concatenate([hi, lo, s[16:24] + e[16:24]], axis=0)
    out_ref[...] = jnp.broadcast_to(out[None], (RING, 24, H))


def sum_parts(received):
    return pl.pallas_call(
        sum_kernel,
        out_shape=jax.ShapeDtypeStruct((RING, 24, H), F32),
        compiler_params=pltpu.CompilerParams(vmem_limit_bytes=VMEM),
        name="sum_parts",
    )(received)


def eliminate(g, b):
    sub = lax.broadcasted_iota(jnp.int32, (8, H), 0)
    group, slack, depth = 2, 2, 1
    blocks = N // 8
    half = blocks // 2

    def groups_of(t):
        return [(g, 0), (g, 1), (b, 0)] if t < half else [(g, 1), (b, 0), (b, 1)]

    def spread(rows, groups, column):
        q = [i for i, (ref, p) in enumerate(groups) if ref is g and p == column // H][0]
        lane = column % H
        return jnp.broadcast_to(rows[q][:, lane : lane + 1], (8, H))

    def over(x, j):
        return jnp.broadcast_to(x[j : j + 1, :], (8, H))

    x, done = [], []
    for t in range(blocks):
        window = group - t % group + slack
        groups = groups_of(t)
        wide = [w for w in range(window) if t + w < blocks]
        rows = [
            [ref[8 * (t + w) : 8 * (t + w) + 8, H * p : H * p + H] for ref, p in groups] for w in wide
        ]
        for w in wide[len(x) :]:
            x.append([spread(rows[w], groups, 8 * t + k) for k in range(8)])
        near = wide[1 : 1 + depth]
        ahead = [None] + [[spread(rows[w], groups, 8 * t + 8 + k) for k in range(8)] for w in near]
        d = over(x[0][0], 0)
        scale = jnp.zeros((8, H), F32)
        for k in range(8):
            r = pltpu.reciprocal(d, approx=True)
            scale = jnp.where(sub == k, lax.rsqrt(d), scale)
            if k < 7:
                corner = over(x[0][k], k + 1)
                d = over(x[0][k + 1], k + 1) - (corner * corner) * r
            u = [x[w][k] * r for w in wide]
            for j in range(k + 1, 8):
                f = over(u[0], j)
                for w in wide:
                    x[w][j] = x[w][j] - x[w][k] * f
            if near:
                for j in range(8):
                    f = over(u[1], j)
                    for w in near:
                        ahead[w][j] = ahead[w][j] - x[w][k] * f
            u[0] = jnp.where(sub > k, u[0], F32(0.0))
            for q in range(3):
                line = over(rows[0][q], k)
                for w in wide:
                    rows[w][q] = rows[w][q] - u[w] * line
        rows[0] = [piece * scale for piece in rows[0]]
        for w in wide:
            for q, (ref, p) in enumerate(groups):
                ref[8 * (t + w) : 8 * (t + w) + 8, H * p : H * p + H] = rows[w][q]
        x = ahead[1:]
        done.append(jnp.concatenate(rows[0], axis=1))
        first = 8 * (t + 1 + slack)
        if t % group < group - 1:
            continue
        if first < N:
            u1, u2, u3 = split3(jnp.concatenate(done, axis=0))
            left = jnp.concatenate([u1, u1, u2, u1, u2, u3], axis=0)
            right = jnp.concatenate([u1, u2, u1, u3, u2, u1], axis=0)
            for part in range(2):
                top, end = max(first, H * part), H * part + H
                if top >= end:
                    continue
                q = [i for i, (ref, p) in enumerate(groups) if ref is g and p == part][0]
                change = dot_t(left[:, H * q : H * q + H], right)
                for i, (ref, p) in enumerate(groups):
                    stop = min(end, H + 8 * (group + slack)) if ref is g and p < part else end
                    if top < stop:
                        ref[top:stop, H * p : H * p + H] -= change[
                            top - H * part : stop - H * part, H * i : H * i + H
                        ]
        done = []


def product3(dot, a, b):
    return dot(a[0], b[0]) + (dot(a[0], b[1]) + dot(a[1], b[0]))


def split2(x):
    one = x.astype(BF16)
    return one, (x - one.astype(F32)).astype(BF16)


STRIP = 512


def factor_kernel(
    core_ref, own_ref, other_ref, panel_hbm, trailing_hbm, factor_hbm, proj_hbm, rest_hbm,
    panel, trailing, rest, factor_ref, proj_ref, hi, lo, g, b, xs, qs, in_sems, out_sems,
):
    loads = (
        pltpu.make_async_copy(panel_hbm, panel, in_sems.at[0]),
        pltpu.make_async_copy(trailing_hbm, trailing, in_sems.at[1]),
    )
    for copy in loads:
        copy.start()
    first_core = core_ref[0] == 0
    for ref, at in ((hi, 0), (lo, 8)):
        mine = own_ref[:, at : at + 8, :].reshape(N, H)
        theirs = other_ref[:, at : at + 8, :].reshape(N, H)
        ref[:, 0:H] = jnp.where(first_core, mine, theirs)
        ref[:, H:N] = jnp.where(first_core, theirs, mine)
    c = own_ref[:, 16:24, :].reshape(N, H)
    g[...] = hi[...]
    row = lax.broadcasted_iota(jnp.int32, (N, N), 0)
    col = lax.broadcasted_iota(jnp.int32, (N, N), 1)
    b[...] = jnp.where(row == col, F32(1.0), F32(0.0))
    eliminate(g, b)

    upper = jnp.where(row <= col, g[...], F32(0.0))
    inverse = jnp.where(row >= col, b[...], F32(0.0))
    w1, w2, w3 = split3(inverse)
    y = product6s(dot_n, (w1, w2, w3), split3(c))
    u1, u2, u3 = grid_split(upper, 7)
    exact = dot_t(u1, u1)
    v = (dot_t(u1, u2) + dot_t(u1, u3)) + (dot_t(u2, u2 * BF16(0.5)) + dot_t(u2, u3))
    d = ((hi[...] - exact) + lo[...]) - (v + v.T)
    f = product3(dot_n, (w1, w2), split2(d))
    e = product3(dot_r, split2(f), (w1, w2))
    size = jnp.max(jnp.sum(jnp.abs(e), axis=0, keepdims=True))
    lower = jnp.where(row > col, F32(1.0), jnp.where(row == col, F32(0.5), F32(0.0)))
    es = split2(e)
    ee = product3(dot_n, es, es)
    q = y - product3(dot_n, es, split2(y))
    q = q + product3(dot_n, split2(ee), split2(q))
    x = e * lower
    xb = split2(x)
    x = (e - product3(dot_r, xb, xb)) * lower
    xs[...] = x
    qs[...] = q

    @pl.when(jnp.logical_not(size < F32(0.03)))
    def _():
        def again(state):
            old, _, count = state
            new = (e - product6(dot_r, old, old)) * lower
            return new, jnp.max(jnp.abs(new - old)), count + 1

        x, _, _ = lax.while_loop(
            lambda s: jnp.logical_and(s[1] > F32(1e-6), s[2] < 60), again, (xs[...], F32(1.0), jnp.int32(0))
        )
        q, power = y, -e
        for _ in range(6):
            q = q + product6(dot_n, power, q)
            power = product6(dot_n, power, power)
        xs[...] = x
        qs[...] = q

    q = qs[...]
    xb = split2(xs[...])
    z1, z2, z3 = split3(product6s(dot_t, (w1, w2, w3), split3(q)))
    proj_ref[...] = q + product3(dot_t, xb, split2(q))
    factor_ref[...] = upper + product3(dot_t, xb, split2(upper))
    strips = panel.shape[0] // STRIP
    stores = [
        pltpu.make_async_copy(factor_ref, factor_hbm, out_sems.at[strips]),
        pltpu.make_async_copy(proj_ref, proj_hbm, out_sems.at[strips + 1]),
    ]
    for copy in stores:
        copy.start()
    zero = jnp.zeros_like(z1)
    right = jnp.concatenate(
        [
            jnp.concatenate(pair, axis=1)
            for pair in ((z1, z2), (z3, zero), (z1, z2), (z1, zero))
        ],
        axis=0,
    )
    for copy in loads:
        copy.wait()
    for i in range(strips):
        rows = slice(i * STRIP, i * STRIP + STRIP)
        a1, a2, a3 = split3(panel[rows, :])
        both = dot_n(jnp.concatenate([a1, a1, a2, a3], axis=1), right)
        rest[rows, :] = trailing[rows, :] - (both[:, 0:H] + both[:, H:N])
        store = pltpu.make_async_copy(rest.at[rows], rest_hbm.at[rows], out_sems.at[i])
        store.start()
        stores.append(store)
    for copy in stores:
        copy.wait()


def factor(core, own, other, panel, trailing):
    rows = panel.shape[0]
    return pl.pallas_call(
        factor_kernel,
        in_specs=[pl.BlockSpec(memory_space=pltpu.SMEM)]
        + [pl.BlockSpec(memory_space=pltpu.VMEM)] * 2
        + [pl.BlockSpec(memory_space=pl.ANY)] * 2,
        out_specs=[pl.BlockSpec(memory_space=pl.ANY)] * 3,
        out_shape=(
            jax.ShapeDtypeStruct((N, N), F32),
            jax.ShapeDtypeStruct((N, H), F32),
            jax.ShapeDtypeStruct((rows, H), F32),
        ),
        scratch_shapes=[
            pltpu.VMEM((rows, N), F32),
            pltpu.VMEM((rows, H), F32),
            pltpu.VMEM((rows, H), F32),
            pltpu.VMEM((N, N), F32),
            pltpu.VMEM((N, H), F32),
            pltpu.VMEM((N, N), F32),
            pltpu.VMEM((N, N), F32),
            pltpu.VMEM((N, N), F32),
            pltpu.VMEM((N, N), F32),
            pltpu.VMEM((N, N), F32),
            pltpu.VMEM((N, H), F32),
            pltpu.SemaphoreType.DMA((2,)),
            pltpu.SemaphoreType.DMA((rows // STRIP + 2,)),
        ],
        compiler_params=pltpu.CompilerParams(vmem_limit_bytes=VMEM),
        name="factor",
    )(core, own, other, panel, trailing)


def on_device(panel, trailing):
    core = lax.axis_index("cols").astype(jnp.int32).reshape(1) % 2
    sent = gram(core, panel, trailing)
    received = lax.all_to_all(sent, "rows", 0, 0, tiled=True)
    summed = sum_parts(received)
    own = lax.all_to_all(summed, "rows", 0, 0, tiled=True)
    other = lax.ppermute(own, "cols", [(j, j ^ 1) for j in range(lax.axis_size("cols"))])
    return tuple(factor(core, own, other, panel, trailing))


def solution(mesh):
    return jax.shard_map(
        on_device,
        mesh=mesh,
        in_specs=(P("rows", None), P("rows", "cols")),
        out_specs=(P(), P(None, "cols"), P("rows", "cols")),
        check_vma=False,
    )
```

```python
import jax
import jax.numpy as jnp
from jax import lax
from jax.experimental import pallas as pl
from jax.experimental.pallas import tpu as pltpu
from jax.sharding import PartitionSpec as P

F32 = jnp.float32
BF16 = jnp.bfloat16
N = 256
H = 128
RING = 32
VMEM = 48 * 1024 * 1024


def dot_t(a, b):
    return lax.dot_general(a, b, (((0,), (0,)), ((), ())), preferred_element_type=F32)


def dot_n(a, b):
    return lax.dot_general(a, b, (((1,), (0,)), ((), ())), preferred_element_type=F32)


def dot_r(a, b):
    return lax.dot_general(a, b, (((1,), (1,)), ((), ())), preferred_element_type=F32)


def split3(x):
    one = x.astype(BF16)
    rest = x - one.astype(F32)
    two = rest.astype(BF16)
    three = (rest - two.astype(F32)).astype(BF16)
    return one, two, three


def product6s(dot, a, b):
    small = (dot(a[0], b[2]) + dot(a[2], b[0])) + dot(a[1], b[1])
    return dot(a[0], b[0]) + ((dot(a[0], b[1]) + dot(a[1], b[0])) + small)


def product6(dot, a, b):
    return product6s(dot, split3(a), split3(b))


def power_near(x):
    big = x * F32(2.0**23 + 1.0)
    return big - (big - x)


def grid_split(x, bits):
    top = jnp.max(jnp.abs(x), axis=0, keepdims=True)
    magic = power_near(top) * F32(1.5 * 2.0 ** (23 - bits))
    coarse = (x + magic) - magic
    rest = x - coarse
    two = rest.astype(BF16)
    three = (rest - two.astype(F32)).astype(BF16)
    return coarse.astype(BF16), two, three


def two_sum(a, b):
    s = a + b
    t = s - a
    return s, (a - (s - t)) + (b - t)


CHUNK = 1024


def gram_kernel(core_ref, panel_hbm, trailing_hbm, out_ref, panel, trailing, sems):
    height = panel.shape[0]
    chunks = height // CHUNK

    def copies(i, start, size):
        rows = pl.ds(start, size)
        return (
            pltpu.make_async_copy(panel_hbm.at[rows], panel.at[rows], sems.at[0, i]),
            pltpu.make_async_copy(trailing_hbm.at[rows], trailing.at[rows], sems.at[1, i]),
        )

    first = copies(0, 0, CHUNK)
    later = copies(1, CHUNK, height - CHUNK)
    for copy in first + later:
        copy.start()
    first_core = core_ref[0] == 0

    def split(i):
        rows = slice(i * CHUNK, i * CHUNK + CHUNK)
        a = grid_split(panel[rows, :], 6)
        t = split3(trailing[rows, :])
        b = [
            (
                jnp.concatenate([x[:, 0:H], y], axis=1),
                jnp.concatenate([jnp.where(first_core, x[:, 0:H], x[:, H:N]), y], axis=1),
            )
            for x, y in zip(a, t)
        ]
        return a, b

    def halves(a, *b):
        return jnp.concatenate(
            [dot_t(a[:, 0:H], jnp.concatenate([x[0] for x in b], axis=1)), dot_t(a[:, H:N], jnp.concatenate([x[1] for x in b], axis=1))],
            axis=0,
        )

    for copy in first:
        copy.wait()
    held = split(0)
    for copy in later:
        copy.wait()
    hi = lo = rest = mixed = jnp.zeros((N, N), F32)
    for i in range(chunks):
        (a1, a2, a3), (b1, b2, b3) = held
        if i + 1 < chunks:
            held = split(i + 1)
        one = halves(a1, b1, b2, b3)
        two = halves(a2, b1, b2, (a3, a3))
        rest = rest + (one[:, N : 2 * N] + one[:, 2 * N :] + (two[:, 0:N] + two[:, N : 2 * N] + halves(a3, b1)))
        mixed = mixed + two[:, 2 * N :]
        hi, e = two_sum(hi, one[:, 0:N])
        lo = lo + e
    mixed = mixed + mixed.T
    mixed = jnp.concatenate(
        [mixed[0:H, 0:H], jnp.where(first_core, mixed[H:N, 0:H], mixed[H:N, H:N])], axis=0
    )
    s, e = two_sum(hi[:, 0:H], rest[:, 0:H] + mixed)
    out_ref[:, 0:8, :] = s.reshape(RING, 8, H)
    out_ref[:, 8:16, :] = (lo[:, 0:H] + e).reshape(RING, 8, H)
    out_ref[:, 16:24, :] = (hi[:, H:N] + (lo[:, H:N] + rest[:, H:N])).reshape(RING, 8, H)


def gram(core, panel, trailing):
    rows = panel.shape[0]
    return pl.pallas_call(
        gram_kernel,
        in_specs=[
            pl.BlockSpec(memory_space=pltpu.SMEM),
            pl.BlockSpec(memory_space=pl.ANY),
            pl.BlockSpec(memory_space=pl.ANY),
        ],
        out_specs=pl.BlockSpec(memory_space=pltpu.VMEM),
        out_shape=jax.ShapeDtypeStruct((RING, 24, H), F32),
        scratch_shapes=[
            pltpu.VMEM((rows, N), F32),
            pltpu.VMEM((rows, H), F32),
            pltpu.SemaphoreType.DMA((2, 2)),
        ],
        compiler_params=pltpu.CompilerParams(vmem_limit_bytes=105 * 512 * 1024),
        name="products",
    )(core, panel, trailing)


def sum_kernel(in_ref, out_ref):
    parts = [(in_ref[d], None) for d in range(RING)]
    while len(parts) > 1:
        merged = []
        for (a, ea), (b, eb) in zip(parts[::2], parts[1::2]):
            s, e = two_sum(a, b)
            if ea is not None:
                e = e + (ea + eb)
            merged.append((s, e))
        parts = merged
    s, e = parts[0]
    hi, lo = two_sum(s[0:8], s[8:16] + e[0:8])
    out = jnp.concatenate([hi, lo, s[16:24] + e[16:24]], axis=0)
    out_ref[...] = jnp.broadcast_to(out[None], (RING, 24, H))


def sum_parts(received):
    return pl.pallas_call(
        sum_kernel,
        out_shape=jax.ShapeDtypeStruct((RING, 24, H), F32),
        compiler_params=pltpu.CompilerParams(vmem_limit_bytes=VMEM),
        name="sum_parts",
    )(received)


def eliminate(g, b):
    group, slack, depth = 2, 2, 1
    sub = lax.broadcasted_iota(jnp.int32, (8, H), 0)
    blocks = H // 8

    def spread(rows, column):
        return jnp.broadcast_to(rows[0][:, column : column + 1], (8, H))

    def over(x, j):
        return jnp.broadcast_to(x[j : j + 1, :], (8, H))

    x, done = [], []
    for t in range(blocks):
        window = group - t % group + slack
        wide = [w for w in range(window) if t + w < blocks]
        rows = [[ref[8 * (t + w) : 8 * (t + w) + 8, :] for ref in (g, b)] for w in wide]
        for w in wide[len(x) :]:
            x.append([spread(rows[w], 8 * t + k) for k in range(8)])
        near = wide[1 : 1 + depth]
        ahead = [None] + [[spread(rows[w], 8 * t + 8 + k) for k in range(8)] for w in near]
        d = over(x[0][0], 0)
        scale = jnp.zeros((8, H), F32)
        for k in range(8):
            r = pltpu.reciprocal(d, approx=True)
            scale = jnp.where(sub == k, lax.rsqrt(d), scale)
            if k < 7:
                corner = over(x[0][k], k + 1)
                d = over(x[0][k + 1], k + 1) - (corner * corner) * r
            u = [x[w][k] * r for w in wide]
            for j in range(k + 1, 8):
                f = over(u[0], j)
                for w in wide:
                    x[w][j] = x[w][j] - x[w][k] * f
            if near:
                for j in range(8):
                    f = over(u[1], j)
                    for w in near:
                        ahead[w][j] = ahead[w][j] - x[w][k] * f
            u[0] = jnp.where(sub > k, u[0], F32(0.0))
            for q in range(2):
                line = over(rows[0][q], k)
                for w in wide:
                    rows[w][q] = rows[w][q] - u[w] * line
        rows[0] = [piece * scale for piece in rows[0]]
        for w in wide:
            for q, ref in enumerate((g, b)):
                ref[8 * (t + w) : 8 * (t + w) + 8, :] = rows[w][q]
        x = ahead[1:]
        done.append(jnp.concatenate(rows[0], axis=1))
        if t % group < group - 1:
            continue
        first = 8 * (t + 1 + slack)
        if first < H:
            u1, u2, u3 = split3(jnp.concatenate(done, axis=0))
            left = jnp.concatenate([u1, u1, u2, u1, u2, u3], axis=0)
            right = jnp.concatenate([u1, u2, u1, u3, u2, u1], axis=0)
            change = dot_t(left[:, 0:H], right)
            g[first:H, :] -= change[first:H, 0:H]
            b[first:H, :] -= change[first:H, H:N]
        done = []


def triangles(g, b):
    row = lax.broadcasted_iota(jnp.int32, (H, H), 0)
    col = lax.broadcasted_iota(jnp.int32, (H, H), 1)
    return jnp.where(row <= col, g[...], F32(0.0)), jnp.where(row >= col, b[...], F32(0.0))


def identity():
    row = lax.broadcasted_iota(jnp.int32, (H, H), 0)
    col = lax.broadcasted_iota(jnp.int32, (H, H), 1)
    return jnp.where(row == col, F32(1.0), F32(0.0))


def first_kernel(own_ref, out_ref, g, b):
    g[...] = own_ref[0 : RING // 2, 0:8, :].reshape(H, H)
    b[...] = identity()
    eliminate(g, b)
    out_ref[0], out_ref[1] = triangles(g, b)


def first_half(own):
    return pl.pallas_call(
        first_kernel,
        out_shape=jax.ShapeDtypeStruct((2, H, H), F32),
        scratch_shapes=[pltpu.VMEM((H, H), F32)] * 2,
        compiler_params=pltpu.CompilerParams(vmem_limit_bytes=VMEM),
        cost_estimate=pl.CostEstimate(flops=40_000_000, bytes_accessed=10_000_000, transcendentals=0),
        name="first_half",
    )(own)


def product3(dot, a, b):
    return dot(a[0], b[0]) + (dot(a[0], b[1]) + dot(a[1], b[0]))


def split2(x):
    one = x.astype(BF16)
    return one, (x - one.astype(F32)).astype(BF16)


STRIP = 512


def factor_kernel(
    core_ref, own_ref, other_ref, first_ref, panel_hbm, trailing_hbm, factor_hbm, proj_hbm, rest_hbm,
    panel, trailing, rest, factor_ref, proj_ref, g, b, xs, qs, in_sems, out_sems,
):
    loads = (
        pltpu.make_async_copy(panel_hbm, panel, in_sems.at[0]),
        pltpu.make_async_copy(trailing_hbm, trailing, in_sems.at[1]),
    )
    for copy in loads:
        copy.start()
    first_core = core_ref[0] == 0
    quarters = []
    for at in (0, 8):
        mine = own_ref[:, at : at + 8, :].reshape(N, H)
        theirs = other_ref[:, at : at + 8, :].reshape(N, H)[H:N]
        top, mine = mine[0:H], mine[H:N]
        quarters.append((top, jnp.where(first_core, mine, theirs), jnp.where(first_core, theirs, mine)))
    (hi00, hi10, hi11), (lo00, lo10, lo11) = quarters
    c = own_ref[:, 16:24, :].reshape(N, H)
    row = lax.broadcasted_iota(jnp.int32, (N, N), 0)
    col = lax.broadcasted_iota(jnp.int32, (N, N), 1)
    u00, w00 = first_ref[0], first_ref[1]
    w00s = split3(w00)
    u01 = product6s(dot_r, w00s, split3(hi10))
    u01s = split3(u01)
    g[...] = hi11 - product6s(dot_t, u01s, u01s)
    b[...] = identity()
    eliminate(g, b)
    u11, w11 = triangles(g, b)
    w10 = -product6(dot_n, w11, product6s(dot_t, u01s, w00s))
    zero = jnp.zeros((H, H), F32)

    def whole(a00, a01, a10, a11):
        return jnp.concatenate(
            [jnp.concatenate([a00, a01], axis=1), jnp.concatenate([a10, a11], axis=1)], axis=0
        )

    upper = whole(u00, u01, zero, u11)
    inverse = whole(w00, zero, w10, w11)
    w1, w2, w3 = split3(inverse)
    y = product6s(dot_n, (w1, w2, w3), split3(c))
    u1, u2, u3 = grid_split(upper, 7)
    exact = dot_t(u1, u1)
    v = (dot_t(u1, u2) + dot_t(u1, u3)) + (dot_t(u2, u2 * BF16(0.5)) + dot_t(u2, u3))
    v = v + v.T
    d00 = ((hi00 - exact[0:H, 0:H]) + lo00) - v[0:H, 0:H]
    d10 = ((hi10 - exact[H:N, 0:H]) + lo10) - v[H:N, 0:H]
    d11 = ((hi11 - exact[H:N, H:N]) + lo11) - v[H:N, H:N]
    d = whole(d00, d10.T, d10, d11)
    f = product3(dot_n, (w1, w2), split2(d))
    e = product3(dot_r, split2(f), (w1, w2))
    miss = product6s(dot_r, (w1, w2, w3), split3(upper)) - jnp.where(row == col, F32(1.0), F32(0.0))
    e = e + (miss + miss.T)
    size = jnp.max(jnp.sum(jnp.abs(e), axis=0, keepdims=True))
    lower = jnp.where(row > col, F32(1.0), jnp.where(row == col, F32(0.5), F32(0.0)))
    es = split2(e)
    ee = product3(dot_n, es, es)
    q = y - product3(dot_n, es, split2(y))
    q = q + product3(dot_n, split2(ee), split2(q))
    x = e * lower
    xb = split2(x)
    x = (e - product3(dot_r, xb, xb)) * lower
    xs[...] = x
    qs[...] = q

    @pl.when(jnp.logical_not(size < F32(0.03)))
    def _():
        def again(state):
            old, _, count = state
            new = (e - product6(dot_r, old, old)) * lower
            return new, jnp.max(jnp.abs(new - old)), count + 1

        x, _, _ = lax.while_loop(
            lambda s: jnp.logical_and(s[1] > F32(1e-6), s[2] < 60), again, (xs[...], F32(1.0), jnp.int32(0))
        )
        q, power = y, -e
        for _ in range(6):
            q = q + product6(dot_n, power, q)
            power = product6(dot_n, power, power)
        xs[...] = x
        qs[...] = q

    q = qs[...]
    xb = split2(xs[...] - miss)
    z1, z2, z3 = split3(product6s(dot_t, (w1, w2, w3), split3(q)))
    proj_ref[...] = q + product3(dot_t, split2(xs[...]), split2(q))
    factor_ref[...] = upper + product3(dot_t, xb, split2(upper))
    strips = panel.shape[0] // STRIP
    stores = [
        pltpu.make_async_copy(factor_ref, factor_hbm, out_sems.at[strips]),
        pltpu.make_async_copy(proj_ref, proj_hbm, out_sems.at[strips + 1]),
    ]
    for copy in stores:
        copy.start()
    zero = jnp.zeros_like(z1)
    right = jnp.concatenate(
        [
            jnp.concatenate(pair, axis=1)
            for pair in ((z1, z2), (z3, zero), (z1, z2), (z1, zero))
        ],
        axis=0,
    )
    for copy in loads:
        copy.wait()
    for i in range(strips):
        rows = slice(i * STRIP, i * STRIP + STRIP)
        a1, a2, a3 = split3(panel[rows, :])
        both = dot_n(jnp.concatenate([a1, a1, a2, a3], axis=1), right)
        rest[rows, :] = trailing[rows, :] - (both[:, 0:H] + both[:, H:N])
        store = pltpu.make_async_copy(rest.at[rows], rest_hbm.at[rows], out_sems.at[i])
        store.start()
        stores.append(store)
    for copy in stores:
        copy.wait()


def factor(core, own, other, first, panel, trailing):
    rows = panel.shape[0]
    return pl.pallas_call(
        factor_kernel,
        in_specs=[pl.BlockSpec(memory_space=pltpu.SMEM)]
        + [pl.BlockSpec(memory_space=pltpu.VMEM)] * 3
        + [pl.BlockSpec(memory_space=pl.ANY)] * 2,
        out_specs=[pl.BlockSpec(memory_space=pl.ANY)] * 3,
        out_shape=(
            jax.ShapeDtypeStruct((N, N), F32),
            jax.ShapeDtypeStruct((N, H), F32),
            jax.ShapeDtypeStruct((rows, H), F32),
        ),
        scratch_shapes=[
            pltpu.VMEM((rows, N), F32),
            pltpu.VMEM((rows, H), F32),
            pltpu.VMEM((rows, H), F32),
            pltpu.VMEM((N, N), F32),
            pltpu.VMEM((N, H), F32),
            pltpu.VMEM((H, H), F32),
            pltpu.VMEM((H, H), F32),
            pltpu.VMEM((N, N), F32),
            pltpu.VMEM((N, H), F32),
            pltpu.SemaphoreType.DMA((2,)),
            pltpu.SemaphoreType.DMA((rows // STRIP + 2,)),
        ],
        compiler_params=pltpu.CompilerParams(vmem_limit_bytes=VMEM),
        name="factor",
    )(core, own, other, first, panel, trailing)


def on_device(panel, trailing):
    core = lax.axis_index("cols").astype(jnp.int32).reshape(1) % 2
    sent = gram(core, panel, trailing)
    received = lax.all_to_all(sent, "rows", 0, 0, tiled=True)
    summed = sum_parts(received)
    own = lax.all_to_all(summed, "rows", 0, 0, tiled=True)
    other = lax.ppermute(own, "cols", [(j, j ^ 1) for j in range(lax.axis_size("cols"))])
    first = first_half(own)
    return tuple(factor(core, own, other, first, panel, trailing))


def solution(mesh):
    return jax.shard_map(
        on_device,
        mesh=mesh,
        in_specs=(P("rows", None), P("rows", "cols")),
        out_specs=(P(), P(None, "cols"), P("rows", "cols")),
        check_vma=False,
    )
```

```python
import jax
import jax.numpy as jnp
from jax import lax
from jax.experimental import pallas as pl
from jax.experimental.pallas import tpu as pltpu
from jax.sharding import PartitionSpec as P

F32 = jnp.float32
BF16 = jnp.bfloat16
N = 256
H = 128
RING = 32
VMEM = 48 * 1024 * 1024


def dot_t(a, b):
    return lax.dot_general(a, b, (((0,), (0,)), ((), ())), preferred_element_type=F32)


def dot_n(a, b):
    return lax.dot_general(a, b, (((1,), (0,)), ((), ())), preferred_element_type=F32)


def dot_r(a, b):
    return lax.dot_general(a, b, (((1,), (1,)), ((), ())), preferred_element_type=F32)


def split3(x):
    one = x.astype(BF16)
    rest = x - one.astype(F32)
    two = rest.astype(BF16)
    three = (rest - two.astype(F32)).astype(BF16)
    return one, two, three


def product6s(dot, a, b):
    small = (dot(a[0], b[2]) + dot(a[2], b[0])) + dot(a[1], b[1])
    return dot(a[0], b[0]) + ((dot(a[0], b[1]) + dot(a[1], b[0])) + small)


def product6(dot, a, b):
    return product6s(dot, split3(a), split3(b))


def power_near(x):
    big = x * F32(2.0**23 + 1.0)
    return big - (big - x)


def grid_split(x, bits):
    top = jnp.max(jnp.abs(x), axis=0, keepdims=True)
    magic = power_near(top) * F32(1.5 * 2.0 ** (23 - bits))
    coarse = (x + magic) - magic
    rest = x - coarse
    two = rest.astype(BF16)
    three = (rest - two.astype(F32)).astype(BF16)
    return coarse.astype(BF16), two, three


def two_sum(a, b):
    s = a + b
    t = s - a
    return s, (a - (s - t)) + (b - t)


CHUNK = 1024


def gram_kernel(core_ref, panel_hbm, trailing_hbm, out_ref, panel, trailing, sems):
    height = panel.shape[0]
    chunks = height // CHUNK

    def copies(i, start, size):
        rows = pl.ds(start, size)
        return (
            pltpu.make_async_copy(panel_hbm.at[rows], panel.at[rows], sems.at[0, i]),
            pltpu.make_async_copy(trailing_hbm.at[rows], trailing.at[rows], sems.at[1, i]),
        )

    first = copies(0, 0, CHUNK)
    later = copies(1, CHUNK, height - CHUNK)
    for copy in first + later:
        copy.start()
    first_core = core_ref[0] == 0

    def split(i):
        rows = slice(i * CHUNK, i * CHUNK + CHUNK)
        a = grid_split(panel[rows, :], 6)
        t = split3(trailing[rows, :])
        b = [
            (
                jnp.concatenate([x[:, 0:H], y], axis=1),
                jnp.concatenate([jnp.where(first_core, x[:, 0:H], x[:, H:N]), y], axis=1),
            )
            for x, y in zip(a, t)
        ]
        return a, b

    def halves(a, *b):
        return jnp.concatenate(
            [dot_t(a[:, 0:H], jnp.concatenate([x[0] for x in b], axis=1)), dot_t(a[:, H:N], jnp.concatenate([x[1] for x in b], axis=1))],
            axis=0,
        )

    for copy in first:
        copy.wait()
    held = split(0)
    for copy in later:
        copy.wait()
    hi = lo = rest = mixed = jnp.zeros((N, N), F32)
    for i in range(chunks):
        (a1, a2, a3), (b1, b2, b3) = held
        if i + 1 < chunks:
            held = split(i + 1)
        one = halves(a1, b1, b2, b3)
        two = halves(a2, b1, b2, (a3, a3))
        rest = rest + (one[:, N : 2 * N] + one[:, 2 * N :] + (two[:, 0:N] + two[:, N : 2 * N] + halves(a3, b1)))
        mixed = mixed + two[:, 2 * N :]
        hi, e = two_sum(hi, one[:, 0:N])
        lo = lo + e
    mixed = mixed + mixed.T
    mixed = jnp.concatenate(
        [mixed[0:H, 0:H], jnp.where(first_core, mixed[H:N, 0:H], mixed[H:N, H:N])], axis=0
    )
    s, e = two_sum(hi[:, 0:H], rest[:, 0:H] + mixed)
    out_ref[:, 0:8, :] = s.reshape(RING, 8, H)
    out_ref[:, 8:16, :] = (lo[:, 0:H] + e).reshape(RING, 8, H)
    out_ref[:, 16:24, :] = (hi[:, H:N] + (lo[:, H:N] + rest[:, H:N])).reshape(RING, 8, H)


def gram(core, panel, trailing):
    rows = panel.shape[0]
    return pl.pallas_call(
        gram_kernel,
        in_specs=[
            pl.BlockSpec(memory_space=pltpu.SMEM),
            pl.BlockSpec(memory_space=pl.ANY),
            pl.BlockSpec(memory_space=pl.ANY),
        ],
        out_specs=pl.BlockSpec(memory_space=pltpu.VMEM),
        out_shape=jax.ShapeDtypeStruct((RING, 24, H), F32),
        scratch_shapes=[
            pltpu.VMEM((rows, N), F32),
            pltpu.VMEM((rows, H), F32),
            pltpu.SemaphoreType.DMA((2, 2)),
        ],
        compiler_params=pltpu.CompilerParams(vmem_limit_bytes=105 * 512 * 1024),
        name="products",
    )(core, panel, trailing)


def sum_kernel(in_ref, out_ref):
    parts = [(in_ref[d], None) for d in range(RING)]
    while len(parts) > 1:
        merged = []
        for (a, ea), (b, eb) in zip(parts[::2], parts[1::2]):
            s, e = two_sum(a, b)
            if ea is not None:
                e = e + (ea + eb)
            merged.append((s, e))
        parts = merged
    s, e = parts[0]
    hi, lo = two_sum(s[0:8], s[8:16] + e[0:8])
    out = jnp.concatenate([hi, lo, s[16:24] + e[16:24]], axis=0)
    out_ref[...] = jnp.broadcast_to(out[None], (RING, 24, H))


def sum_parts(received):
    return pl.pallas_call(
        sum_kernel,
        out_shape=jax.ShapeDtypeStruct((RING, 24, H), F32),
        compiler_params=pltpu.CompilerParams(vmem_limit_bytes=VMEM),
        name="sum_parts",
    )(received)


def eliminate(g, b):
    group, slack, depth = 2, 2, 1
    sub = lax.broadcasted_iota(jnp.int32, (8, H), 0)
    blocks = H // 8

    def spread(rows, column):
        return jnp.broadcast_to(rows[0][:, column : column + 1], (8, H))

    def over(x, j):
        return jnp.broadcast_to(x[j : j + 1, :], (8, H))

    x, done = [], []
    for t in range(blocks):
        window = group - t % group + slack
        wide = [w for w in range(window) if t + w < blocks]
        rows = [[ref[8 * (t + w) : 8 * (t + w) + 8, :] for ref in (g, b)] for w in wide]
        for w in wide[len(x) :]:
            x.append([spread(rows[w], 8 * t + k) for k in range(8)])
        near = wide[1 : 1 + depth]
        ahead = [None] + [[spread(rows[w], 8 * t + 8 + k) for k in range(8)] for w in near]
        d = over(x[0][0], 0)
        scale = jnp.zeros((8, H), F32)
        for k in range(8):
            r = pltpu.reciprocal(d, approx=True)
            scale = jnp.where(sub == k, lax.rsqrt(d), scale)
            if k < 7:
                corner = over(x[0][k], k + 1)
                d = over(x[0][k + 1], k + 1) - (corner * corner) * r
            u = [x[w][k] * r for w in wide]
            for j in range(k + 1, 8):
                f = over(u[0], j)
                for w in wide:
                    x[w][j] = x[w][j] - x[w][k] * f
            if near:
                for j in range(8):
                    f = over(u[1], j)
                    for w in near:
                        ahead[w][j] = ahead[w][j] - x[w][k] * f
            u[0] = jnp.where(sub > k, u[0], F32(0.0))
            for q in range(2):
                line = over(rows[0][q], k)
                for w in wide:
                    rows[w][q] = rows[w][q] - u[w] * line
        rows[0] = [piece * scale for piece in rows[0]]
        for w in wide:
            for q, ref in enumerate((g, b)):
                ref[8 * (t + w) : 8 * (t + w) + 8, :] = rows[w][q]
        x = ahead[1:]
        done.append(jnp.concatenate(rows[0], axis=1))
        if t % group < group - 1:
            continue
        first = 8 * (t + 1 + slack)
        if first < H:
            u1, u2, u3 = split3(jnp.concatenate(done, axis=0))
            left = jnp.concatenate([u1, u1, u2, u1, u2, u3], axis=0)
            right = jnp.concatenate([u1, u2, u1, u3, u2, u1], axis=0)
            change = dot_t(left[:, 0:H], right)
            g[first:H, :] -= change[first:H, 0:H]
            b[first:H, :] -= change[first:H, H:N]
        done = []


def triangles(g, b):
    row = lax.broadcasted_iota(jnp.int32, (H, H), 0)
    col = lax.broadcasted_iota(jnp.int32, (H, H), 1)
    return jnp.where(row <= col, g[...], F32(0.0)), jnp.where(row >= col, b[...], F32(0.0))


def identity():
    row = lax.broadcasted_iota(jnp.int32, (H, H), 0)
    col = lax.broadcasted_iota(jnp.int32, (H, H), 1)
    return jnp.where(row == col, F32(1.0), F32(0.0))


def first_kernel(own_ref, out_ref, g, b):
    g[...] = own_ref[0 : RING // 2, 0:8, :].reshape(H, H)
    b[...] = identity()
    eliminate(g, b)
    out_ref[0], out_ref[1] = triangles(g, b)


def first_half(own):
    return pl.pallas_call(
        first_kernel,
        out_shape=jax.ShapeDtypeStruct((2, H, H), F32),
        scratch_shapes=[pltpu.VMEM((H, H), F32)] * 2,
        compiler_params=pltpu.CompilerParams(vmem_limit_bytes=VMEM),
        cost_estimate=pl.CostEstimate(flops=40_000_000, bytes_accessed=10_000_000, transcendentals=0),
        name="first_half",
    )(own)


def product3(dot, a, b):
    return dot(a[0], b[0]) + (dot(a[0], b[1]) + dot(a[1], b[0]))


def split2(x):
    one = x.astype(BF16)
    return one, (x - one.astype(F32)).astype(BF16)


STRIP = 512


def factor_kernel(
    core_ref, own_ref, other_ref, first_ref, panel_hbm, trailing_hbm, factor_hbm, proj_hbm, rest_hbm,
    panel, trailing, rest, factor_ref, proj_ref, g, b, xs, qs, in_sems, out_sems,
):
    loads = (
        pltpu.make_async_copy(panel_hbm, panel, in_sems.at[0]),
        pltpu.make_async_copy(trailing_hbm, trailing, in_sems.at[1]),
    )
    for copy in loads:
        copy.start()
    first_core = core_ref[0] == 0
    quarters = []
    for at in (0, 8):
        mine = own_ref[:, at : at + 8, :].reshape(N, H)
        theirs = other_ref[:, at : at + 8, :].reshape(N, H)[H:N]
        top, mine = mine[0:H], mine[H:N]
        quarters.append((top, jnp.where(first_core, mine, theirs), jnp.where(first_core, theirs, mine)))
    (hi00, hi10, hi11), (lo00, lo10, lo11) = quarters
    c = own_ref[:, 16:24, :].reshape(N, H)
    row = lax.broadcasted_iota(jnp.int32, (N, N), 0)
    col = lax.broadcasted_iota(jnp.int32, (N, N), 1)
    u00, w00 = first_ref[0], first_ref[1]
    w00s = split3(w00)
    u01 = product6s(dot_r, w00s, split3(hi10))
    u01s = split3(u01)
    g[...] = hi11 - product6s(dot_t, u01s, u01s)
    b[...] = identity()
    eliminate(g, b)
    u11, w11 = triangles(g, b)
    w10 = -product6(dot_n, w11, product6s(dot_t, u01s, w00s))
    zero = jnp.zeros((H, H), F32)

    def whole(a00, a01, a10, a11):
        return jnp.concatenate(
            [jnp.concatenate([a00, a01], axis=1), jnp.concatenate([a10, a11], axis=1)], axis=0
        )

    upper = whole(u00, u01, zero, u11)
    inverse = whole(w00, zero, w10, w11)
    w1, w2, w3 = split3(inverse)
    y = product6s(dot_n, (w1, w2, w3), split3(c))
    u1, u2, u3 = grid_split(upper, 7)
    exact = dot_t(u1, u1)
    v = (dot_t(u1, u2) + dot_t(u1, u3)) + (dot_t(u2, u2 * BF16(0.5)) + dot_t(u2, u3))
    v = v + v.T
    d00 = ((hi00 - exact[0:H, 0:H]) + lo00) - v[0:H, 0:H]
    d10 = ((hi10 - exact[H:N, 0:H]) + lo10) - v[H:N, 0:H]
    d11 = ((hi11 - exact[H:N, H:N]) + lo11) - v[H:N, H:N]
    d = whole(d00, d10.T, d10, d11)
    f = product3(dot_n, (w1, w2), split2(d))
    e = product3(dot_r, split2(f), (w1, w2))
    miss = product6s(dot_r, (w1, w2, w3), split3(upper)) - jnp.where(row == col, F32(1.0), F32(0.0))
    e = e + (miss + miss.T)
    size = jnp.sum(jnp.sum(e * e, axis=0, keepdims=True))
    lower = jnp.where(row > col, F32(1.0), jnp.where(row == col, F32(0.5), F32(0.0)))
    es = split2(e)
    ee = product3(dot_n, es, es)
    q = y - product3(dot_n, es, split2(y))
    q = q + product3(dot_n, split2(ee), split2(q))
    x = e * lower
    xb = split2(x)
    x = (e - product3(dot_r, xb, xb)) * lower
    xs[...] = x
    qs[...] = q

    @pl.when(jnp.logical_not(size < F32(0.05**2)))
    def _():
        def again(state):
            old, _, count = state
            new = (e - product6(dot_r, old, old)) * lower
            return new, jnp.max(jnp.abs(new - old)), count + 1

        x, _, _ = lax.while_loop(
            lambda s: jnp.logical_and(s[1] > F32(1e-6), s[2] < 60), again, (xs[...], F32(1.0), jnp.int32(0))
        )
        q, power = y, -e
        for _ in range(6):
            q = q + product6(dot_n, power, q)
            power = product6(dot_n, power, power)
        xs[...] = x
        qs[...] = q

    q = qs[...]
    xb = split2(xs[...] - miss)
    z1, z2, z3 = split3(product6s(dot_t, (w1, w2, w3), split3(q)))
    proj_ref[...] = q + product3(dot_t, split2(xs[...]), split2(q))
    factor_ref[...] = upper + product3(dot_t, xb, split2(upper))
    strips = panel.shape[0] // STRIP
    stores = [
        pltpu.make_async_copy(factor_ref, factor_hbm, out_sems.at[strips]),
        pltpu.make_async_copy(proj_ref, proj_hbm, out_sems.at[strips + 1]),
    ]
    for copy in stores:
        copy.start()
    zero = jnp.zeros_like(z1)
    right = jnp.concatenate(
        [
            jnp.concatenate(pair, axis=1)
            for pair in ((z1, z2), (z3, zero), (z1, z2), (z1, zero))
        ],
        axis=0,
    )
    for copy in loads:
        copy.wait()
    for i in range(strips):
        rows = slice(i * STRIP, i * STRIP + STRIP)
        a1, a2, a3 = split3(panel[rows, :])
        both = dot_n(jnp.concatenate([a1, a1, a2, a3], axis=1), right)
        rest[rows, :] = trailing[rows, :] - (both[:, 0:H] + both[:, H:N])
        store = pltpu.make_async_copy(rest.at[rows], rest_hbm.at[rows], out_sems.at[i])
        store.start()
        stores.append(store)
    for copy in stores:
        copy.wait()


def factor(core, own, other, first, panel, trailing):
    rows = panel.shape[0]
    return pl.pallas_call(
        factor_kernel,
        in_specs=[pl.BlockSpec(memory_space=pltpu.SMEM)]
        + [pl.BlockSpec(memory_space=pltpu.VMEM)] * 3
        + [pl.BlockSpec(memory_space=pl.ANY)] * 2,
        out_specs=[pl.BlockSpec(memory_space=pl.ANY)] * 3,
        out_shape=(
            jax.ShapeDtypeStruct((N, N), F32),
            jax.ShapeDtypeStruct((N, H), F32),
            jax.ShapeDtypeStruct((rows, H), F32),
        ),
        scratch_shapes=[
            pltpu.VMEM((rows, N), F32),
            pltpu.VMEM((rows, H), F32),
            pltpu.VMEM((rows, H), F32),
            pltpu.VMEM((N, N), F32),
            pltpu.VMEM((N, H), F32),
            pltpu.VMEM((H, H), F32),
            pltpu.VMEM((H, H), F32),
            pltpu.VMEM((N, N), F32),
            pltpu.VMEM((N, H), F32),
            pltpu.SemaphoreType.DMA((2,)),
            pltpu.SemaphoreType.DMA((rows // STRIP + 2,)),
        ],
        compiler_params=pltpu.CompilerParams(vmem_limit_bytes=VMEM),
        name="factor",
    )(core, own, other, first, panel, trailing)


def on_device(panel, trailing):
    core = lax.axis_index("cols").astype(jnp.int32).reshape(1) % 2
    sent = gram(core, panel, trailing)
    received = lax.all_to_all(sent, "rows", 0, 0, tiled=True)
    summed = sum_parts(received)
    own = lax.all_to_all(summed, "rows", 0, 0, tiled=True)
    other = lax.ppermute(own, "cols", [(j, j ^ 1) for j in range(lax.axis_size("cols"))])
    first = first_half(own)
    return tuple(factor(core, own, other, first, panel, trailing))


def solution(mesh):
    return jax.shard_map(
        on_device,
        mesh=mesh,
        in_specs=(P("rows", None), P("rows", "cols")),
        out_specs=(P(), P(None, "cols"), P("rows", "cols")),
        check_vma=False,
    )
```

```python
import jax
import jax.numpy as jnp
from jax import lax
from jax.experimental import pallas as pl
from jax.experimental.pallas import tpu as pltpu
from jax.sharding import PartitionSpec as P

F32 = jnp.float32
BF16 = jnp.bfloat16
N = 256
H = 128
RING = 32
VMEM = 48 * 1024 * 1024


def dot_t(a, b):
    return lax.dot_general(a, b, (((0,), (0,)), ((), ())), preferred_element_type=F32)


def dot_n(a, b):
    return lax.dot_general(a, b, (((1,), (0,)), ((), ())), preferred_element_type=F32)


def dot_r(a, b):
    return lax.dot_general(a, b, (((1,), (1,)), ((), ())), preferred_element_type=F32)


def split3(x):
    one = x.astype(BF16)
    rest = x - one.astype(F32)
    two = rest.astype(BF16)
    three = (rest - two.astype(F32)).astype(BF16)
    return one, two, three


def product6s(dot, a, b):
    small = (dot(a[0], b[2]) + dot(a[2], b[0])) + dot(a[1], b[1])
    return dot(a[0], b[0]) + ((dot(a[0], b[1]) + dot(a[1], b[0])) + small)


def product6(dot, a, b):
    return product6s(dot, split3(a), split3(b))


def power_near(x):
    big = x * F32(2.0**23 + 1.0)
    return big - (big - x)


def grid_split(x, bits):
    top = jnp.max(jnp.abs(x), axis=0, keepdims=True)
    magic = power_near(top) * F32(1.5 * 2.0 ** (23 - bits))
    coarse = (x + magic) - magic
    rest = x - coarse
    two = rest.astype(BF16)
    three = (rest - two.astype(F32)).astype(BF16)
    return coarse.astype(BF16), two, three


def two_sum(a, b):
    s = a + b
    t = s - a
    return s, (a - (s - t)) + (b - t)


CHUNK = 1024


def gram_kernel(core_ref, panel_hbm, trailing_hbm, out_ref, panel, trailing, sems):
    height = panel.shape[0]
    chunks = height // CHUNK

    def copies(i, start, size):
        rows = pl.ds(start, size)
        return (
            pltpu.make_async_copy(panel_hbm.at[rows], panel.at[rows], sems.at[0, i]),
            pltpu.make_async_copy(trailing_hbm.at[rows], trailing.at[rows], sems.at[1, i]),
        )

    first = copies(0, 0, CHUNK)
    later = copies(1, CHUNK, height - CHUNK)
    for copy in first + later:
        copy.start()
    first_core = core_ref[0] == 0

    def split(i):
        rows = slice(i * CHUNK, i * CHUNK + CHUNK)
        a = grid_split(panel[rows, :], 6)
        t = split3(trailing[rows, :])
        b = [
            (
                jnp.concatenate([x[:, 0:H], y], axis=1),
                jnp.concatenate([jnp.where(first_core, x[:, 0:H], x[:, H:N]), y], axis=1),
            )
            for x, y in zip(a, t)
        ]
        return a, b

    def halves(a, *b):
        return jnp.concatenate(
            [dot_t(a[:, 0:H], jnp.concatenate([x[0] for x in b], axis=1)), dot_t(a[:, H:N], jnp.concatenate([x[1] for x in b], axis=1))],
            axis=0,
        )

    for copy in first:
        copy.wait()
    held = split(0)
    for copy in later:
        copy.wait()
    hi = lo = rest = mixed = jnp.zeros((N, N), F32)
    for i in range(chunks):
        (a1, a2, a3), (b1, b2, b3) = held
        if i + 1 < chunks:
            held = split(i + 1)
        one = halves(a1, b1, b2, b3)
        two = halves(a2, b1, b2, (a3, a3))
        rest = rest + (one[:, N : 2 * N] + one[:, 2 * N :] + (two[:, 0:N] + two[:, N : 2 * N] + halves(a3, b1)))
        mixed = mixed + two[:, 2 * N :]
        hi, e = two_sum(hi, one[:, 0:N])
        lo = lo + e
    mixed = mixed + mixed.T
    mixed = jnp.concatenate(
        [mixed[0:H, 0:H], jnp.where(first_core, mixed[H:N, 0:H], mixed[H:N, H:N])], axis=0
    )
    s, e = two_sum(hi[:, 0:H], rest[:, 0:H] + mixed)
    out_ref[:, 0:8, :] = s.reshape(RING, 8, H)
    out_ref[:, 8:16, :] = (lo[:, 0:H] + e).reshape(RING, 8, H)
    out_ref[:, 16:24, :] = (hi[:, H:N] + (lo[:, H:N] + rest[:, H:N])).reshape(RING, 8, H)


def gram(core, panel, trailing):
    rows = panel.shape[0]
    return pl.pallas_call(
        gram_kernel,
        in_specs=[
            pl.BlockSpec(memory_space=pltpu.SMEM),
            pl.BlockSpec(memory_space=pl.ANY),
            pl.BlockSpec(memory_space=pl.ANY),
        ],
        out_specs=pl.BlockSpec(memory_space=pltpu.VMEM),
        out_shape=jax.ShapeDtypeStruct((RING, 24, H), F32),
        scratch_shapes=[
            pltpu.VMEM((rows, N), F32),
            pltpu.VMEM((rows, H), F32),
            pltpu.SemaphoreType.DMA((2, 2)),
        ],
        compiler_params=pltpu.CompilerParams(vmem_limit_bytes=105 * 512 * 1024),
        name="products",
    )(core, panel, trailing)


def sum_kernel(in_ref, out_ref):
    parts = [(in_ref[d], None) for d in range(RING)]
    while len(parts) > 1:
        merged = []
        for (a, ea), (b, eb) in zip(parts[::2], parts[1::2]):
            s, e = two_sum(a, b)
            if ea is not None:
                e = e + (ea + eb)
            merged.append((s, e))
        parts = merged
    s, e = parts[0]
    hi, lo = two_sum(s[0:8], s[8:16] + e[0:8])
    out = jnp.concatenate([hi, lo, s[16:24] + e[16:24]], axis=0)
    out_ref[...] = jnp.broadcast_to(out[None], (RING, 24, H))


def sum_parts(received):
    return pl.pallas_call(
        sum_kernel,
        out_shape=jax.ShapeDtypeStruct((RING, 24, H), F32),
        compiler_params=pltpu.CompilerParams(vmem_limit_bytes=VMEM),
        name="sum_parts",
    )(received)


def eliminate(g, b):
    group, slack, depth = 2, 2, 1
    sub = lax.broadcasted_iota(jnp.int32, (8, H), 0)
    blocks = H // 8

    def spread(rows, column):
        return jnp.broadcast_to(rows[0][:, column : column + 1], (8, H))

    def over(x, j):
        return jnp.broadcast_to(x[j : j + 1, :], (8, H))

    x, done = [], []
    for t in range(blocks):
        window = group - t % group + slack
        wide = [w for w in range(window) if t + w < blocks]
        rows = [[ref[8 * (t + w) : 8 * (t + w) + 8, :] for ref in (g, b)] for w in wide]
        for w in wide[len(x) :]:
            x.append([spread(rows[w], 8 * t + k) for k in range(8)])
        near = wide[1 : 1 + depth]
        ahead = [None] + [[spread(rows[w], 8 * t + 8 + k) for k in range(8)] for w in near]
        d = over(x[0][0], 0)
        scale = jnp.zeros((8, H), F32)
        for k in range(8):
            r = pltpu.reciprocal(d, approx=True)
            scale = jnp.where(sub == k, lax.rsqrt(d), scale)
            if k < 7:
                corner = over(x[0][k], k + 1)
                d = over(x[0][k + 1], k + 1) - (corner * corner) * r
            u = [x[w][k] * r for w in wide]
            for j in range(k + 1, 8):
                f = over(u[0], j)
                for w in wide:
                    x[w][j] = x[w][j] - x[w][k] * f
            if near:
                for j in range(8):
                    f = over(u[1], j)
                    for w in near:
                        ahead[w][j] = ahead[w][j] - x[w][k] * f
            u[0] = jnp.where(sub > k, u[0], F32(0.0))
            for q in range(2):
                line = over(rows[0][q], k)
                for w in wide:
                    rows[w][q] = rows[w][q] - u[w] * line
        rows[0] = [piece * scale for piece in rows[0]]
        for w in wide:
            for q, ref in enumerate((g, b)):
                ref[8 * (t + w) : 8 * (t + w) + 8, :] = rows[w][q]
        x = ahead[1:]
        done.append(jnp.concatenate(rows[0], axis=1))
        if t % group < group - 1:
            continue
        first = 8 * (t + 1 + slack)
        if first < H:
            u1, u2, u3 = split3(jnp.concatenate(done, axis=0))
            left = jnp.concatenate([u1, u1, u2, u1, u2, u3], axis=0)
            right = jnp.concatenate([u1, u2, u1, u3, u2, u1], axis=0)
            change = dot_t(left[:, 0:H], right)
            g[first:H, :] -= change[first:H, 0:H]
            b[first:H, :] -= change[first:H, H:N]
        done = []


def triangles(g, b):
    row = lax.broadcasted_iota(jnp.int32, (H, H), 0)
    col = lax.broadcasted_iota(jnp.int32, (H, H), 1)
    return jnp.where(row <= col, g[...], F32(0.0)), jnp.where(row >= col, b[...], F32(0.0))


def identity():
    row = lax.broadcasted_iota(jnp.int32, (H, H), 0)
    col = lax.broadcasted_iota(jnp.int32, (H, H), 1)
    return jnp.where(row == col, F32(1.0), F32(0.0))


def first_kernel(top_ref, out_ref, g, b):
    g[...] = top_ref[...].reshape(H, H)
    b[...] = identity()
    eliminate(g, b)
    out_ref[0], out_ref[1] = triangles(g, b)


def first_half(own):
    return pl.pallas_call(
        first_kernel,
        grid=(1,),
        in_specs=[pl.BlockSpec((RING // 2, 8, H), lambda i: (0, 0, 0))],
        out_specs=pl.BlockSpec((2, H, H), lambda i: (0, 0, 0)),
        out_shape=jax.ShapeDtypeStruct((2, H, H), F32),
        scratch_shapes=[pltpu.VMEM((H, H), F32)] * 2,
        compiler_params=pltpu.CompilerParams(vmem_limit_bytes=VMEM),
        cost_estimate=pl.CostEstimate(flops=40_000_000, bytes_accessed=10_000_000, transcendentals=0),
        name="first_half",
    )(own)


def product3(dot, a, b):
    return dot(a[0], b[0]) + (dot(a[0], b[1]) + dot(a[1], b[0]))


def split2(x):
    one = x.astype(BF16)
    return one, (x - one.astype(F32)).astype(BF16)


STRIP = 512


def factor_kernel(
    core_ref, own_ref, other_ref, first_ref, panel_hbm, trailing_hbm, factor_hbm, proj_hbm, rest_hbm,
    panel, trailing, rest, factor_ref, proj_ref, g, b, xs, qs, in_sems, out_sems,
):
    loads = (
        pltpu.make_async_copy(panel_hbm, panel, in_sems.at[0]),
        pltpu.make_async_copy(trailing_hbm, trailing, in_sems.at[1]),
    )
    for copy in loads:
        copy.start()
    first_core = core_ref[0] == 0
    quarters = []
    for at in (0, 8):
        mine = own_ref[:, at : at + 8, :].reshape(N, H)
        theirs = other_ref[:, at : at + 8, :].reshape(H, H)
        top, mine = mine[0:H], mine[H:N]
        quarters.append((top, jnp.where(first_core, mine, theirs), jnp.where(first_core, theirs, mine)))
    (hi00, hi10, hi11), (lo00, lo10, lo11) = quarters
    c = own_ref[:, 16:24, :].reshape(N, H)
    row = lax.broadcasted_iota(jnp.int32, (N, N), 0)
    col = lax.broadcasted_iota(jnp.int32, (N, N), 1)
    u00, w00 = first_ref[0], first_ref[1]
    w00s = split3(w00)
    u01 = product6s(dot_r, w00s, split3(hi10))
    u01s = split3(u01)
    g[...] = hi11 - product6s(dot_t, u01s, u01s)
    b[...] = identity()
    eliminate(g, b)
    u11, w11 = triangles(g, b)
    w10 = -product6(dot_n, w11, product6s(dot_t, u01s, w00s))
    zero = jnp.zeros((H, H), F32)

    def whole(a00, a01, a10, a11):
        return jnp.concatenate(
            [jnp.concatenate([a00, a01], axis=1), jnp.concatenate([a10, a11], axis=1)], axis=0
        )

    upper = whole(u00, u01, zero, u11)
    inverse = whole(w00, zero, w10, w11)
    w1, w2, w3 = split3(inverse)
    y = product6s(dot_n, (w1, w2, w3), split3(c))
    u1, u2, u3 = grid_split(upper, 7)
    exact = dot_t(u1, u1)
    v = (dot_t(u1, u2) + dot_t(u1, u3)) + (dot_t(u2, u2 * BF16(0.5)) + dot_t(u2, u3))
    v = v + v.T
    d00 = ((hi00 - exact[0:H, 0:H]) + lo00) - v[0:H, 0:H]
    d10 = ((hi10 - exact[H:N, 0:H]) + lo10) - v[H:N, 0:H]
    d11 = ((hi11 - exact[H:N, H:N]) + lo11) - v[H:N, H:N]
    d = whole(d00, d10.T, d10, d11)
    f = product3(dot_n, (w1, w2), split2(d))
    e = product3(dot_r, split2(f), (w1, w2))
    miss = product6s(dot_r, (w1, w2, w3), split3(upper)) - jnp.where(row == col, F32(1.0), F32(0.0))
    e = e + (miss + miss.T)
    size = jnp.sum(jnp.sum(e * e, axis=0, keepdims=True))
    lower = jnp.where(row > col, F32(1.0), jnp.where(row == col, F32(0.5), F32(0.0)))
    es = split2(e)
    ee = product3(dot_n, es, es)
    q = y - product3(dot_n, es, split2(y))
    q = q + product3(dot_n, split2(ee), split2(q))
    x = e * lower
    xb = split2(x)
    x = (e - product3(dot_r, xb, xb)) * lower
    xs[...] = x
    qs[...] = q

    @pl.when(jnp.logical_not(size < F32(0.05**2)))
    def _():
        def again(state):
            old, _, count = state
            new = (e - product6(dot_r, old, old)) * lower
            return new, jnp.max(jnp.abs(new - old)), count + 1

        x, _, _ = lax.while_loop(
            lambda s: jnp.logical_and(s[1] > F32(1e-6), s[2] < 60), again, (xs[...], F32(1.0), jnp.int32(0))
        )
        q, power = y, -e
        for _ in range(6):
            q = q + product6(dot_n, power, q)
            power = product6(dot_n, power, power)
        xs[...] = x
        qs[...] = q

    q = qs[...]
    xb = split2(xs[...] - miss)
    z1, z2, z3 = split3(product6s(dot_t, (w1, w2, w3), split3(q)))
    proj_ref[...] = q + product3(dot_t, split2(xs[...]), split2(q))
    factor_ref[...] = upper + product3(dot_t, xb, split2(upper))
    strips = panel.shape[0] // STRIP
    stores = [
        pltpu.make_async_copy(factor_ref, factor_hbm, out_sems.at[strips]),
        pltpu.make_async_copy(proj_ref, proj_hbm, out_sems.at[strips + 1]),
    ]
    for copy in stores:
        copy.start()
    zero = jnp.zeros_like(z1)
    right = jnp.concatenate(
        [
            jnp.concatenate(pair, axis=1)
            for pair in ((z1, z2), (z3, zero), (z1, z2), (z1, zero))
        ],
        axis=0,
    )
    for copy in loads:
        copy.wait()
    for i in range(strips):
        rows = slice(i * STRIP, i * STRIP + STRIP)
        a1, a2, a3 = split3(panel[rows, :])
        both = dot_n(jnp.concatenate([a1, a1, a2, a3], axis=1), right)
        rest[rows, :] = trailing[rows, :] - (both[:, 0:H] + both[:, H:N])
        store = pltpu.make_async_copy(rest.at[rows], rest_hbm.at[rows], out_sems.at[i])
        store.start()
        stores.append(store)
    for copy in stores:
        copy.wait()


def factor(core, own, other, first, panel, trailing):
    rows = panel.shape[0]
    return pl.pallas_call(
        factor_kernel,
        grid=(1,),
        in_specs=[pl.BlockSpec(memory_space=pltpu.SMEM)]
        + [
            pl.BlockSpec(memory_space=pltpu.VMEM),
            pl.BlockSpec((RING // 2, 16, H), lambda i: (1, 0, 0)),
            pl.BlockSpec(memory_space=pltpu.VMEM),
        ]
        + [pl.BlockSpec(memory_space=pl.ANY)] * 2,
        out_specs=[pl.BlockSpec(memory_space=pl.ANY)] * 3,
        out_shape=(
            jax.ShapeDtypeStruct((N, N), F32),
            jax.ShapeDtypeStruct((N, H), F32),
            jax.ShapeDtypeStruct((rows, H), F32),
        ),
        scratch_shapes=[
            pltpu.VMEM((rows, N), F32),
            pltpu.VMEM((rows, H), F32),
            pltpu.VMEM((rows, H), F32),
            pltpu.VMEM((N, N), F32),
            pltpu.VMEM((N, H), F32),
            pltpu.VMEM((H, H), F32),
            pltpu.VMEM((H, H), F32),
            pltpu.VMEM((N, N), F32),
            pltpu.VMEM((N, H), F32),
            pltpu.SemaphoreType.DMA((2,)),
            pltpu.SemaphoreType.DMA((rows // STRIP + 2,)),
        ],
        compiler_params=pltpu.CompilerParams(vmem_limit_bytes=VMEM),
        name="factor",
    )(core, own, other, first, panel, trailing)


def on_device(panel, trailing):
    core = lax.axis_index("cols").astype(jnp.int32).reshape(1) % 2
    sent = gram(core, panel, trailing)
    received = lax.all_to_all(sent, "rows", 0, 0, tiled=True)
    summed = sum_parts(received)
    own = lax.all_to_all(summed, "rows", 0, 0, tiled=True)
    other = lax.ppermute(own, "cols", [(j, j ^ 1) for j in range(lax.axis_size("cols"))])
    first = first_half(own)
    return tuple(factor(core, own, other, first, panel, trailing))


def solution(mesh):
    return jax.shard_map(
        on_device,
        mesh=mesh,
        in_specs=(P("rows", None), P("rows", "cols")),
        out_specs=(P(), P(None, "cols"), P("rows", "cols")),
        check_vma=False,
    )
```

```python
import jax
import jax.numpy as jnp
from jax import lax
from jax.experimental import pallas as pl
from jax.experimental.pallas import tpu as pltpu
from jax.sharding import PartitionSpec as P

F32 = jnp.float32
BF16 = jnp.bfloat16
N = 256
H = 128
RING = 32
VMEM = 48 * 1024 * 1024


def dot_t(a, b):
    return lax.dot_general(a, b, (((0,), (0,)), ((), ())), preferred_element_type=F32)


def dot_n(a, b):
    return lax.dot_general(a, b, (((1,), (0,)), ((), ())), preferred_element_type=F32)


def dot_r(a, b):
    return lax.dot_general(a, b, (((1,), (1,)), ((), ())), preferred_element_type=F32)


def split3(x):
    one = x.astype(BF16)
    rest = x - one.astype(F32)
    two = rest.astype(BF16)
    three = (rest - two.astype(F32)).astype(BF16)
    return one, two, three


def product6s(dot, a, b):
    small = (dot(a[0], b[2]) + dot(a[2], b[0])) + dot(a[1], b[1])
    return dot(a[0], b[0]) + ((dot(a[0], b[1]) + dot(a[1], b[0])) + small)


def product6(dot, a, b):
    return product6s(dot, split3(a), split3(b))


def power_near(x):
    big = x * F32(2.0**23 + 1.0)
    return big - (big - x)


def grid_split(x, bits):
    top = jnp.max(jnp.abs(x), axis=0, keepdims=True)
    magic = power_near(top) * F32(1.5 * 2.0 ** (23 - bits))
    coarse = (x + magic) - magic
    rest = x - coarse
    two = rest.astype(BF16)
    three = (rest - two.astype(F32)).astype(BF16)
    return coarse.astype(BF16), two, three


def two_sum(a, b):
    s = a + b
    t = s - a
    return s, (a - (s - t)) + (b - t)


CHUNK = 1024


def gram_kernel(core_ref, panel_hbm, trailing_hbm, out_ref, panel, trailing, sems):
    height = panel.shape[0]
    chunks = height // CHUNK

    def copies(i, start, size):
        rows = pl.ds(start, size)
        return (
            pltpu.make_async_copy(panel_hbm.at[rows], panel.at[rows], sems.at[0, i]),
            pltpu.make_async_copy(trailing_hbm.at[rows], trailing.at[rows], sems.at[1, i]),
        )

    first = copies(0, 0, CHUNK)
    later = copies(1, CHUNK, height - CHUNK)
    for copy in first + later:
        copy.start()
    first_core = core_ref[0] == 0

    def split(i):
        rows = slice(i * CHUNK, i * CHUNK + CHUNK)
        a = grid_split(panel[rows, :], 6)
        t = split3(trailing[rows, :])
        b = [
            (
                jnp.concatenate([x[:, 0:H], y], axis=1),
                jnp.concatenate([jnp.where(first_core, x[:, 0:H], x[:, H:N]), y], axis=1),
            )
            for x, y in zip(a, t)
        ]
        return a, b

    def halves(a, *b):
        return jnp.concatenate(
            [dot_t(a[:, 0:H], jnp.concatenate([x[0] for x in b], axis=1)), dot_t(a[:, H:N], jnp.concatenate([x[1] for x in b], axis=1))],
            axis=0,
        )

    for copy in first:
        copy.wait()
    held = split(0)
    for copy in later:
        copy.wait()
    hi = lo = rest = mixed = jnp.zeros((N, N), F32)
    for i in range(chunks):
        (a1, a2, a3), (b1, b2, b3) = held
        if i + 1 < chunks:
            held = split(i + 1)
        one = halves(a1, b1, b2, b3)
        two = halves(a2, b1, b2, (a3, a3))
        rest = rest + (one[:, N : 2 * N] + one[:, 2 * N :] + (two[:, 0:N] + two[:, N : 2 * N] + halves(a3, b1)))
        mixed = mixed + two[:, 2 * N :]
        hi, e = two_sum(hi, one[:, 0:N])
        lo = lo + e
    mixed = mixed + mixed.T
    mixed = jnp.concatenate(
        [mixed[0:H, 0:H], jnp.where(first_core, mixed[H:N, 0:H], mixed[H:N, H:N])], axis=0
    )
    s, e = two_sum(hi[:, 0:H], rest[:, 0:H] + mixed)
    out_ref[:, 0:8, :] = s.reshape(RING, 8, H)
    out_ref[:, 8:16, :] = (lo[:, 0:H] + e).reshape(RING, 8, H)
    out_ref[:, 16:24, :] = (hi[:, H:N] + (lo[:, H:N] + rest[:, H:N])).reshape(RING, 8, H)


def gram(core, panel, trailing):
    rows = panel.shape[0]
    return pl.pallas_call(
        gram_kernel,
        in_specs=[
            pl.BlockSpec(memory_space=pltpu.SMEM),
            pl.BlockSpec(memory_space=pl.ANY),
            pl.BlockSpec(memory_space=pl.ANY),
        ],
        out_specs=pl.BlockSpec(memory_space=pltpu.VMEM),
        out_shape=jax.ShapeDtypeStruct((RING, 24, H), F32),
        scratch_shapes=[
            pltpu.VMEM((rows, N), F32),
            pltpu.VMEM((rows, H), F32),
            pltpu.SemaphoreType.DMA((2, 2)),
        ],
        compiler_params=pltpu.CompilerParams(vmem_limit_bytes=105 * 512 * 1024),
        name="products",
    )(core, panel, trailing)


def sum_kernel(in_ref, out_ref):
    parts = [(in_ref[d], None) for d in range(RING)]
    while len(parts) > 1:
        merged = []
        for (a, ea), (b, eb) in zip(parts[::2], parts[1::2]):
            s, e = two_sum(a, b)
            if ea is not None:
                e = e + (ea + eb)
            merged.append((s, e))
        parts = merged
    s, e = parts[0]
    hi, lo = two_sum(s[0:8], s[8:16] + e[0:8])
    out = jnp.concatenate([hi, lo, s[16:24] + e[16:24]], axis=0)
    out_ref[...] = jnp.broadcast_to(out[None], (RING, 24, H))


def sum_parts(received):
    return pl.pallas_call(
        sum_kernel,
        out_shape=jax.ShapeDtypeStruct((RING, 24, H), F32),
        compiler_params=pltpu.CompilerParams(vmem_limit_bytes=VMEM),
        name="sum_parts",
    )(received)


def eliminate(g, b):
    group, slack, depth = 2, 2, 1
    sub = lax.broadcasted_iota(jnp.int32, (8, H), 0)
    blocks = H // 8

    def spread(rows, column):
        return jnp.broadcast_to(rows[0][:, column : column + 1], (8, H))

    def over(x, j):
        return jnp.broadcast_to(x[j : j + 1, :], (8, H))

    x, done = [], []
    for t in range(blocks):
        window = group - t % group + slack
        wide = [w for w in range(window) if t + w < blocks]
        rows = [[ref[8 * (t + w) : 8 * (t + w) + 8, :] for ref in (g, b)] for w in wide]
        for w in wide[len(x) :]:
            x.append([spread(rows[w], 8 * t + k) for k in range(8)])
        near = wide[1 : 1 + depth]
        ahead = [None] + [[spread(rows[w], 8 * t + 8 + k) for k in range(8)] for w in near]
        d = over(x[0][0], 0)
        scale = jnp.zeros((8, H), F32)
        for k in range(8):
            r = pltpu.reciprocal(d, approx=True)
            scale = jnp.where(sub == k, lax.rsqrt(d), scale)
            if k < 7:
                corner = over(x[0][k], k + 1)
                d = over(x[0][k + 1], k + 1) - (corner * corner) * r
            u = [x[w][k] * r for w in wide]
            for j in range(k + 1, 8):
                f = over(u[0], j)
                for w in wide:
                    x[w][j] = x[w][j] - x[w][k] * f
            if near:
                for j in range(8):
                    f = over(u[1], j)
                    for w in near:
                        ahead[w][j] = ahead[w][j] - x[w][k] * f
            u[0] = jnp.where(sub > k, u[0], F32(0.0))
            for q in range(2):
                line = over(rows[0][q], k)
                for w in wide:
                    rows[w][q] = rows[w][q] - u[w] * line
        rows[0] = [piece * scale for piece in rows[0]]
        for w in wide:
            for q, ref in enumerate((g, b)):
                ref[8 * (t + w) : 8 * (t + w) + 8, :] = rows[w][q]
        x = ahead[1:]
        done.append(jnp.concatenate(rows[0], axis=1))
        if t % group < group - 1:
            continue
        first = 8 * (t + 1 + slack)
        if first < H:
            u1, u2, u3 = split3(jnp.concatenate(done, axis=0))
            left = jnp.concatenate([u1, u1, u2, u1, u2, u3], axis=0)
            right = jnp.concatenate([u1, u2, u1, u3, u2, u1], axis=0)
            change = dot_t(left[:, 0:H], right)
            g[first:H, :] -= change[first:H, 0:H]
            b[first:H, :] -= change[first:H, H:N]
        done = []


def triangles(g, b):
    row = lax.broadcasted_iota(jnp.int32, (H, H), 0)
    col = lax.broadcasted_iota(jnp.int32, (H, H), 1)
    return jnp.where(row <= col, g[...], F32(0.0)), jnp.where(row >= col, b[...], F32(0.0))


def identity():
    row = lax.broadcasted_iota(jnp.int32, (H, H), 0)
    col = lax.broadcasted_iota(jnp.int32, (H, H), 1)
    return jnp.where(row == col, F32(1.0), F32(0.0))


def first_kernel(own_ref, out_ref, g, b):
    g[...] = own_ref[0 : RING // 2, 0:8, :].reshape(H, H)
    b[...] = identity()
    eliminate(g, b)
    out_ref[0], out_ref[1] = triangles(g, b)


def first_half(own):
    return pl.pallas_call(
        first_kernel,
        out_shape=jax.ShapeDtypeStruct((2, H, H), F32),
        scratch_shapes=[pltpu.VMEM((H, H), F32)] * 2,
        compiler_params=pltpu.CompilerParams(vmem_limit_bytes=VMEM),
        cost_estimate=pl.CostEstimate(flops=40_000_000, bytes_accessed=10_000_000, transcendentals=0),
        name="first_half",
    )(own)


def product3(dot, a, b):
    return dot(a[0], b[0]) + (dot(a[0], b[1]) + dot(a[1], b[0]))


def split2(x):
    one = x.astype(BF16)
    return one, (x - one.astype(F32)).astype(BF16)


STRIP = 512


def factor_kernel(
    core_ref, own_ref, other_ref, first_ref, panel_hbm, trailing_hbm, factor_hbm, proj_hbm, rest_hbm,
    panel, trailing, rest, factor_ref, proj_ref, g, b, xs, qs, in_sems, out_sems,
):
    loads = (
        pltpu.make_async_copy(panel_hbm, panel, in_sems.at[0]),
        pltpu.make_async_copy(trailing_hbm, trailing, in_sems.at[1]),
    )
    for copy in loads:
        copy.start()
    first_core = core_ref[0] == 0
    quarters = []
    for at in (0, 8):
        mine = own_ref[:, at : at + 8, :].reshape(N, H)
        theirs = other_ref[:, at : at + 8, :].reshape(N, H)[H:N]
        top, mine = mine[0:H], mine[H:N]
        quarters.append((top, jnp.where(first_core, mine, theirs), jnp.where(first_core, theirs, mine)))
    (hi00, hi10, hi11), (lo00, lo10, lo11) = quarters
    c = own_ref[:, 16:24, :].reshape(N, H)
    row = lax.broadcasted_iota(jnp.int32, (N, N), 0)
    col = lax.broadcasted_iota(jnp.int32, (N, N), 1)
    u00, w00 = first_ref[0], first_ref[1]
    w00s = split3(w00)
    u01 = product6s(dot_r, w00s, split3(hi10))
    u01s = split3(u01)
    g[...] = hi11 - product6s(dot_t, u01s, u01s)
    b[...] = identity()
    eliminate(g, b)
    u11, w11 = triangles(g, b)
    w10 = -product6(dot_n, w11, product6s(dot_t, u01s, w00s))
    zero = jnp.zeros((H, H), F32)

    def whole(a00, a01, a10, a11):
        return jnp.concatenate(
            [jnp.concatenate([a00, a01], axis=1), jnp.concatenate([a10, a11], axis=1)], axis=0
        )

    upper = whole(u00, u01, zero, u11)
    inverse = whole(w00, zero, w10, w11)
    w1, w2, w3 = split3(inverse)
    y = product6s(dot_n, (w1, w2, w3), split3(c))
    u1, u2, u3 = grid_split(upper, 7)
    exact = dot_t(u1, u1)
    v = (dot_t(u1, u2) + dot_t(u1, u3)) + (dot_t(u2, u2 * BF16(0.5)) + dot_t(u2, u3))
    v = v + v.T
    d00 = ((hi00 - exact[0:H, 0:H]) + lo00) - v[0:H, 0:H]
    d10 = ((hi10 - exact[H:N, 0:H]) + lo10) - v[H:N, 0:H]
    d11 = ((hi11 - exact[H:N, H:N]) + lo11) - v[H:N, H:N]
    d = whole(d00, d10.T, d10, d11)
    f = product3(dot_n, (w1, w2), split2(d))
    e = product3(dot_r, split2(f), (w1, w2))
    miss = product6s(dot_r, (w1, w2, w3), split3(upper)) - jnp.where(row == col, F32(1.0), F32(0.0))
    e = e + (miss + miss.T)
    size = jnp.sum(jnp.sum(e * e, axis=0, keepdims=True))
    lower = jnp.where(row > col, F32(1.0), jnp.where(row == col, F32(0.5), F32(0.0)))
    es = split2(e)
    ee = product3(dot_n, es, es)
    q = y - product3(dot_n, es, split2(y))
    q = q + product3(dot_n, split2(ee), split2(q))
    x = e * lower
    xb = split2(x)
    x = (e - product3(dot_r, xb, xb)) * lower
    xs[...] = x
    qs[...] = q

    @pl.when(jnp.logical_not(size < F32(0.05**2)))
    def _():
        def again(state):
            old, _, count = state
            new = (e - product6(dot_r, old, old)) * lower
            return new, jnp.max(jnp.abs(new - old)), count + 1

        x, _, _ = lax.while_loop(
            lambda s: jnp.logical_and(s[1] > F32(1e-6), s[2] < 60), again, (xs[...], F32(1.0), jnp.int32(0))
        )
        q, power = y, -e
        for _ in range(6):
            q = q + product6(dot_n, power, q)
            power = product6(dot_n, power, power)
        xs[...] = x
        qs[...] = q

    q = qs[...]
    xb = split2(xs[...] - miss)
    z1, z2, z3 = split3(product6s(dot_t, (w1, w2, w3), split3(q)))
    strips = panel.shape[0] // STRIP
    stores = []
    zero = jnp.zeros_like(z1)
    right = jnp.concatenate(
        [
            jnp.concatenate(pair, axis=1)
            for pair in ((z1, z2), (z3, zero), (z1, z2), (z1, zero))
        ],
        axis=0,
    )
    for copy in loads:
        copy.wait()
    for i in range(strips):
        rows = slice(i * STRIP, i * STRIP + STRIP)
        a1, a2, a3 = split3(panel[rows, :])
        both = dot_n(jnp.concatenate([a1, a1, a2, a3], axis=1), right)
        rest[rows, :] = trailing[rows, :] - (both[:, 0:H] + both[:, H:N])
        store = pltpu.make_async_copy(rest.at[rows], rest_hbm.at[rows], out_sems.at[i])
        store.start()
        stores.append(store)
        if i == strips // 2:
            proj_ref[...] = q + product3(dot_t, split2(xs[...]), split2(q))
            factor_ref[...] = upper + product3(dot_t, xb, split2(upper))
            for source, target in ((factor_ref, factor_hbm), (proj_ref, proj_hbm)):
                copy = pltpu.make_async_copy(source, target, out_sems.at[strips + len(stores) - i - 1])
                copy.start()
                stores.append(copy)
    for copy in stores:
        copy.wait()


def factor(core, own, other, first, panel, trailing):
    rows = panel.shape[0]
    return pl.pallas_call(
        factor_kernel,
        in_specs=[pl.BlockSpec(memory_space=pltpu.SMEM)]
        + [pl.BlockSpec(memory_space=pltpu.VMEM)] * 3
        + [pl.BlockSpec(memory_space=pl.ANY)] * 2,
        out_specs=[pl.BlockSpec(memory_space=pl.ANY)] * 3,
        out_shape=(
            jax.ShapeDtypeStruct((N, N), F32),
            jax.ShapeDtypeStruct((N, H), F32),
            jax.ShapeDtypeStruct((rows, H), F32),
        ),
        scratch_shapes=[
            pltpu.VMEM((rows, N), F32),
            pltpu.VMEM((rows, H), F32),
            pltpu.VMEM((rows, H), F32),
            pltpu.VMEM((N, N), F32),
            pltpu.VMEM((N, H), F32),
            pltpu.VMEM((H, H), F32),
            pltpu.VMEM((H, H), F32),
            pltpu.VMEM((N, N), F32),
            pltpu.VMEM((N, H), F32),
            pltpu.SemaphoreType.DMA((2,)),
            pltpu.SemaphoreType.DMA((rows // STRIP + 2,)),
        ],
        compiler_params=pltpu.CompilerParams(vmem_limit_bytes=VMEM),
        name="factor",
    )(core, own, other, first, panel, trailing)


def on_device(panel, trailing):
    core = lax.axis_index("cols").astype(jnp.int32).reshape(1) % 2
    sent = gram(core, panel, trailing)
    received = lax.all_to_all(sent, "rows", 0, 0, tiled=True)
    summed = sum_parts(received)
    own = lax.all_to_all(summed, "rows", 0, 0, tiled=True)
    other = lax.ppermute(own, "cols", [(j, j ^ 1) for j in range(lax.axis_size("cols"))])
    first = first_half(own)
    return tuple(factor(core, own, other, first, panel, trailing))


def solution(mesh):
    return jax.shard_map(
        on_device,
        mesh=mesh,
        in_specs=(P("rows", None), P("rows", "cols")),
        out_specs=(P(), P(None, "cols"), P("rows", "cols")),
        check_vma=False,
    )
```
